256 devices in a mesh: feat: 8 (over y, x_hi), tok: 32 (over z, x_lo, core).
Axes of the slice: x: 4 (x_hi: 2, x_lo: 2; x = x_hi * 2 + x_lo), y: 4, z: 8, core: 2. Of those that a mesh axis runs over, the one named last changes fastest.
Arguments:
- tokens: bfloat16 [8192, 12288], P('tok', 'feat'), may hold values from -6 to 6
- gate_weight: bfloat16 [16, 5, 768, 768], P('feat', None, 'tok'), may hold values from -0.09375 to 0.09375
- up_weight: bfloat16 [16, 5, 768, 768], P('feat', None, 'tok'), may hold values from -0.09375 to 0.09375
- gate_scale: float32 [16, 5], P('feat'), may hold values from 0.35 to 2.8
- up_scale: float32 [16, 5], P('feat'), may hold values from 0.35 to 2.8
- partners: int32 [16, 5], replicated, may hold values from 0 to 15, as said below
- latent_in: bfloat16 [12288, 768], P('feat'), may hold values from -0.0546875 to 0.0546875
- latent_out: bfloat16 [768, 12288], P(None, 'feat'), may hold values from -0.21875 to 0.21875
Outputs:
- hidden: bfloat16 [8192, 12288], P('tok', 'feat')
- rank_term: bfloat16 [8192, 12288], P('tok', 'feat')
The draws below stay inside these ranges and needn't reach their ends.
Inputs may be any that keep to these rules, and one draw needn't show every extreme that they name: `partners`: row i lists the blocks i, i xor 1, i xor 2, i xor 4 and i xor 8, each once, in some order.
All inputs are finite; a program needn't handle non-finite values.
Results may differ from the reference program's by a relative error of at most 0.015.
Values may be sent and summed in bfloat16 or wider, within the bound.
No kernel may reach another device: no remote copies, remote signals or barrier semaphores. Data moves between devices by JAX's collectives and lax.ppermute only.
A program may use at most 128 MiB of HBM per device.

```python
import math
import jax
import jax.numpy as jnp
from jax import lax

BLK = 768
NBLK = 16
PART = 5
RANK = 768
D = 12288
TOKENS = 8192


def draw_partners(key, part):
    row_ids = jnp.arange(NBLK, dtype=jnp.int32)
    offsets = jnp.concatenate([jnp.zeros((1,), jnp.int32), jnp.left_shift(jnp.ones((PART - 1,), jnp.int32), jnp.arange(PART - 1, dtype=jnp.int32))])
    base_ids = jnp.bitwise_xor(row_ids[:, None], offsets[None, :])
    row_keys = jax.random.split(jax.random.fold_in(key, 7), NBLK)
    orders = jax.vmap(lambda row_key: jax.random.permutation(row_key, PART))(row_keys)
    return jnp.take_along_axis(base_ids, orders.astype(jnp.int32), axis=1)


def block_scale(own_key, dims, cuts, least, high):
    factor_of, own = 1.0, jax.random.fold_in(own_key, 6)
    for position, parts in cuts:
        draws = jnp.exp(jax.random.uniform(jax.random.fold_in(own, position), (parts,), jnp.float32, least / len(cuts), high / len(cuts)))
        factor_of = factor_of * jnp.repeat(draws, dims[position] // parts).reshape([-1 if axis == position else 1 for axis in range(len(dims))])
    return factor_of


def centred(rng, shape, deviation, limit, cuts=(), kind=jnp.bfloat16):
    drawn = deviation * jax.random.normal(rng, shape, jnp.float32)
    if cuts:
        drawn = drawn * block_scale(rng, shape, cuts, -0.22, 0.18)
    return jnp.clip(drawn, -limit, limit).astype(kind)


def setup_inputs(seed: int = 0) -> dict:
    key_of = jax.random.split(jax.random.key(seed), 9)
    tokens = centred(key_of[0], (TOKENS, D), 1.0, 6.0, ((0, 32), (1, 8)))
    gate_weight = centred(key_of[1], (NBLK, PART, BLK, BLK), (PART * BLK) ** -0.5, 0.09375, ((0, 8), (2, 32)))
    up_weight = centred(key_of[2], (NBLK, PART, BLK, BLK), (PART * BLK) ** -0.5, 0.09375, ((0, 8), (2, 32)))
    gate_scale = jnp.clip(jnp.exp(math.log(2.8) - 2.0794415 * jax.random.uniform(key_of[3], (NBLK, PART), jnp.float32) ** block_scale(key_of[3], (NBLK, PART), ((0, 8),), -0.2, 0.2)), 0.35, 2.8)
    up_scale = jnp.clip(jnp.exp(math.log(2.8) - 2.0794415 * jax.random.uniform(key_of[4], (NBLK, PART), jnp.float32) ** block_scale(key_of[4], (NBLK, PART), ((0, 8),), -0.2, 0.2)), 0.35, 2.8)
    partners = draw_partners(jax.random.fold_in(key_of[8], 71), 0)
    latent_in = centred(key_of[6], (D, RANK), D ** -0.5, 0.0546875, ((0, 8),))
    latent_out = centred(key_of[7], (RANK, D), RANK ** -0.5, 0.21875, ((1, 8),))
    return dict(tokens=tokens, gate_weight=gate_weight, up_weight=up_weight, gate_scale=gate_scale, up_scale=up_scale, partners=partners, latent_in=latent_in, latent_out=latent_out)


def slot_inputs(tokens, row_ids):
    return jnp.stack([lax.dynamic_slice_in_dim(tokens, (row_ids[slot_idx] * BLK).astype(jnp.int32), BLK, 1) for slot_idx in range(PART)])


def reference(tokens, gate_weight, up_weight, gate_scale, up_scale, partners, latent_in, latent_out):
    def one_block(block_id):
        row_ids = partners[block_id]
        inputs = slot_inputs(tokens, row_ids).astype(jnp.float32)
        gate_terms = jnp.einsum("ktb,kbc->ktc", inputs, gate_weight[block_id].astype(jnp.float32))
        up_terms = jnp.einsum("ktb,kbc->ktc", inputs, up_weight[block_id].astype(jnp.float32))
        gate_sum = jnp.sum(gate_terms * gate_scale[block_id][:, None, None], axis=0)
        up_sum = jnp.sum(up_terms * up_scale[block_id][:, None, None], axis=0)
        return (jax.nn.silu(gate_sum) * up_sum).astype(jnp.bfloat16)

    blocks = lax.map(one_block, jnp.arange(NBLK, dtype=jnp.int32))
    hidden = jnp.transpose(blocks, (1, 0, 2)).reshape(TOKENS, NBLK * BLK)
    latent = jnp.dot(hidden, latent_in, preferred_element_type=jnp.float32).astype(jnp.bfloat16)
    rank_term = jnp.dot(latent, latent_out, preferred_element_type=jnp.float32).astype(jnp.bfloat16)
    return hidden, rank_term
```

```python
import functools
import jax
import jax.numpy as jnp
from jax import lax
from jax.experimental import pallas as pl
from jax.experimental.pallas import tpu as pltpu
from jax.sharding import PartitionSpec as P

GROUP = 4
ANY = pl.BlockSpec(memory_space=pl.ANY)
SMEM = pl.BlockSpec(memory_space=pltpu.SMEM)
VMEM = pl.BlockSpec(memory_space=pltpu.VMEM)
VMEM_BYTES = 44 * 2**20


def swapped(value, axis, mask):
    return lax.ppermute(value, axis, [(i, i ^ mask) for i in range(lax.axis_size(axis))])


def shifted(value, step):
    count = lax.axis_size("tok")
    return lax.ppermute(value, "tok", [(i, (i + step * GROUP) % count) for i in range(count)])


def natural(pieces, own):
    low, high = (own & 1) == 1, (own & 2) == 2
    a = [jnp.where(low, pieces[m ^ 1], pieces[m]) for m in range(4)]
    return [jnp.where(high, a[m ^ 2], a[m]) for m in range(4)]


def gate_up_kernel(cand_ref, gs_ref, us_ref, w_ref, *refs, rows, width):
    s_refs, p_refs, out_ref = refs[:4], refs[4:16], refs[16]
    x_mem, w_mem, g_acc, u_acc, x_sem, w_sem = refs[17:]
    own, blk = cand_ref[5], w_ref.shape[2]
    w_copies = []
    for k in range(5):
        w_copies.append(pltpu.make_async_copy(w_ref.at[:, k], w_mem.at[:, k], w_sem.at[k]))
    x_copies = []
    for m in range(4):
        mine = []
        at = pl.ds(m * rows, rows)
        for j in range(2):
            col = pl.multiple_of((own ^ j) * blk, blk)
            mine.append(pltpu.make_async_copy(s_refs[m].at[:, pl.ds(col, blk)], x_mem.at[j, at], x_sem.at[m, j]))
        for d in range(3):
            mine.append(pltpu.make_async_copy(p_refs[d * 4 + m], x_mem.at[2 + d, at], x_sem.at[m, 2 + d]))
        x_copies.append(mine)
    for m in range(2):
        for copy in x_copies[m]:
            copy.start()
    for copy in w_copies:
        copy.start()
    for m in range(2, 4):
        for copy in x_copies[m]:
            copy.start()
    for half in range(2):
        for m in (2 * half, 2 * half + 1):
            for copy in x_copies[m]:
                copy.wait()
        at = pl.ds(half * 2 * rows, 2 * rows)
        for k in range(5):
            if half == 0:
                w_copies[k].wait()
            x = x_mem[cand_ref[k], at]
            g = jnp.dot(x, w_mem[0, k], preferred_element_type=jnp.float32) * gs_ref[k]
            u = jnp.dot(x, w_mem[1, k], preferred_element_type=jnp.float32) * us_ref[k]
            if k == 0:
                g_acc[...] = g
                u_acc[...] = u
            else:
                g_acc[...] += g
                u_acc[...] += u
        g = g_acc[...]
        out = (g / (1.0 + jnp.exp(-g)) * u_acc[...]).astype(jnp.bfloat16)
        out_ref[2 * half] = out[:rows]
        out_ref[2 * half + 1] = out[rows:]


def gate_up(cand, gs, us, weights, own_rows, partner_rows):
    rows = own_rows[0].shape[0]
    _, slots, blk, width = weights.shape
    flops = 2 * 2 * 4 * rows * slots * blk * width
    return pl.pallas_call(
        functools.partial(gate_up_kernel, rows=rows, width=width),
        out_shape=jax.ShapeDtypeStruct((4, rows, width), jnp.bfloat16),
        in_specs=[SMEM] * 3 + [ANY] * 17,
        out_specs=VMEM,
        scratch_shapes=[
            pltpu.VMEM((slots, 4 * rows, blk), jnp.bfloat16),
            pltpu.VMEM((2, slots, blk, width), jnp.bfloat16),
            pltpu.VMEM((2 * rows, width), jnp.float32),
            pltpu.VMEM((2 * rows, width), jnp.float32),
            pltpu.SemaphoreType.DMA((4, 5)),
            pltpu.SemaphoreType.DMA((5,)),
        ],
        compiler_params=pltpu.CompilerParams(vmem_limit_bytes=VMEM_BYTES),
        cost_estimate=pl.CostEstimate(flops=flops, bytes_accessed=12 * 2**20, transcendentals=4 * rows * width),
    )(cand, gs, us, weights, *own_rows, *partner_rows)


def latent_kernel(own_ref, lin_ref, *refs, wide, narrow):
    a_refs, b_refs, hidden_ref, part_ref = refs[:4], refs[4:8], refs[8], refs[9]
    both = wide + narrow
    total = None
    for m in range(4):
        start = pl.multiple_of((own_ref[0] ^ m) * both, both)
        a, b = a_refs[m][...], b_refs[m][...]
        hidden_ref[:, pl.ds(start, wide)] = a
        hidden_ref[:, pl.ds(pl.multiple_of(start + wide, 128), narrow)] = b
        term = jnp.dot(a, lin_ref[pl.ds(start, wide)], preferred_element_type=jnp.float32)
        term += jnp.dot(b, lin_ref[pl.ds(pl.multiple_of(start + wide, 128), narrow)], preferred_element_type=jnp.float32)
        total = term if total is None else total + term
    part_ref[...] = total.astype(jnp.bfloat16)


def per_device(tokens, gate_weight, up_weight, gate_scale, up_scale, partners, latent_in, latent_out):
    rows, features = tokens.shape
    blocks, slots, share, blk = gate_weight.shape
    feat_count = lax.axis_size("feat")
    z_count = lax.axis_size("tok") // GROUP
    half = blk // 2
    wide = (half // 128 * 2 + 2) // 3 * 128
    cuts = ((0, wide), (wide, half - wide))
    feat, tok = lax.axis_index("feat"), lax.axis_index("tok")
    member, z = tok % GROUP, tok // GROUP
    x_lo, core = member // 2, member % 2
    block_id = feat * blocks + x_lo

    def piece(mask, start, width):
        to = member ^ mask
        parts = [
            lax.dynamic_slice(w, (to // 2, 0, 0, to % 2 * half + start), (1, slots, share, width))
            for w in (gate_weight, up_weight)
        ]
        return jnp.concatenate(parts)

    starts = []
    for start, width in cuts:
        got = [piece(0, start, width)]
        for mask in (1, 2, 3):
            got.append(swapped(piece(mask, start, width), "tok", mask))
        starts.append(jnp.stack(natural(got, member), axis=2).reshape(2, slots, GROUP * share, width))

    def block_of(value):
        return lax.dynamic_slice(value, (0, x_lo * blk), (rows, blk))

    s2 = swapped(tokens, "tok", 2)
    s1 = swapped(tokens, "tok", 1)
    first, second = block_of(tokens), block_of(s2)
    p0 = [swapped(first, "feat", mask) for mask in (1, 2, 4)]
    p2 = [swapped(second, "feat", mask) for mask in (1, 2, 4)]
    s3 = swapped(s2, "tok", 1)
    p1 = [swapped(v, "tok", 1) for v in p0]
    p3 = [swapped(v, "tok", 1) for v in p2]
    own_rows = [tokens, s1, s2, s3]
    partner_rows = [p[d] for d in range(3) for p in (p0, p1, p2, p3)]

    def placed(buffer, value, origin):
        return lax.dynamic_update_slice(buffer, value[:, :, None], (0, 0, origin % z_count, 0, 0))

    full = [placed(jnp.zeros((2, slots, z_count) + v.shape[2:], v.dtype), v, z) for v in starts]
    forward, back = list(starts), list(starts)
    for step in range(1, z_count // 2):
        for i in range(2):
            forward[i] = shifted(forward[i], 1)
            back[i] = shifted(back[i], -1)
            full[i] = placed(full[i], forward[i], z - step + z_count)
            full[i] = placed(full[i], back[i], z + step)
    for i in range(2):
        last = jnp.concatenate([shifted(forward[i][:1], 1), shifted(back[i][1:], -1)])
        full[i] = placed(full[i], last, z + z_count // 2)

    wanted = lax.dynamic_index_in_dim(partners, block_id, 0, keepdims=False)
    labels = block_id ^ jnp.array([0, 1, 2, 4, 8], jnp.int32)
    order = jnp.sum(jnp.where(wanted[:, None] == labels[None, :], jnp.arange(5, dtype=jnp.int32)[None, :], 0), axis=1)
    cand = jnp.concatenate([order, x_lo[None].astype(jnp.int32)])
    gs = lax.dynamic_index_in_dim(gate_scale, x_lo, 0, keepdims=False)
    us = lax.dynamic_index_in_dim(up_scale, x_lo, 0, keepdims=False)

    hidden_pieces = []
    for i in range(2):
        made = gate_up(cand, gs, us, full[i].reshape(2, slots, blk, -1), own_rows, partner_rows)
        hidden_pieces += [made[0]] + [swapped(made[m], "tok", m) for m in (1, 2, 3)]
    hidden, part = pl.pallas_call(
        functools.partial(latent_kernel, wide=cuts[0][1], narrow=cuts[1][1]),
        out_shape=(
            jax.ShapeDtypeStruct((rows, features), jnp.bfloat16),
            jax.ShapeDtypeStruct((rows, latent_in.shape[1]), jnp.bfloat16),
        ),
        in_specs=[SMEM] + [VMEM] * 9,
        out_specs=(VMEM, VMEM),
        compiler_params=pltpu.CompilerParams(vmem_limit_bytes=VMEM_BYTES),
        cost_estimate=pl.CostEstimate(flops=2 * rows * features * latent_in.shape[1], bytes_accessed=4 * 2**20, transcendentals=0),
    )(member[None].astype(jnp.int32), latent_in, *hidden_pieces)

    parts = part.reshape(feat_count, rows // feat_count, -1)
    terms = lax.all_to_all(parts, "feat", 0, 0)
    mine = jnp.sum(terms.astype(jnp.float32), axis=0).astype(jnp.bfloat16)
    latent = lax.all_to_all(jnp.broadcast_to(mine[None], parts.shape), "feat", 0, 0).reshape(rows, -1)
    rank_term = jnp.dot(latent, latent_out, preferred_element_type=jnp.float32).astype(jnp.bfloat16)
    return hidden, rank_term


def solution(mesh):
    placed = (
        P("tok", "feat"),
        P("feat", None, "tok", None),
        P("feat", None, "tok", None),
        P("feat", None),
        P("feat", None),
        P(),
        P("feat", None),
        P(None, "feat"),
    )
    return jax.shard_map(
        per_device,
        mesh=mesh,
        in_specs=placed,
        out_specs=(P("tok", "feat"), P("tok", "feat")),
        check_vma=False,
    )
```

```python
import functools
import jax
import jax.numpy as jnp
from jax import lax
from jax.experimental import pallas as pl
from jax.experimental.pallas import tpu as pltpu
from jax.sharding import PartitionSpec as P

GROUP = 4
HBM = pl.BlockSpec(memory_space=pltpu.HBM)
SMEM = pl.BlockSpec(memory_space=pltpu.SMEM)
VMEM = pl.BlockSpec(memory_space=pltpu.VMEM)
VMEM_BYTES = 44 * 2**20


def swapped(value, axis, mask):
    return lax.ppermute(value, axis, [(i, i ^ mask) for i in range(lax.axis_size(axis))])


def shifted(value, step):
    count = lax.axis_size("tok")
    return lax.ppermute(value, "tok", [(i, (i + step * GROUP) % count) for i in range(count)])


def pack_kernel(own_ref, gate_ref, up_ref, *out_refs):
    half = gate_ref.shape[3] // 2
    for m in range(4):
        to = own_ref[0] ^ m
        at = pl.ds(pl.multiple_of(to % 2 * half, 128), half)
        for side, ref in enumerate((gate_ref, up_ref)):
            out_refs[m][side] = ref[to // 2, :, :, at]


def place_kernel(own_ref, *refs):
    for m in range(4):
        refs[4][:, :, own_ref[0] ^ m] = refs[m][...]


def gate_up_kernel(cand_ref, gs_ref, us_ref, *refs, rows, z_count):
    n_w = z_count + 1
    w_refs, s_refs, p_refs, out_ref = refs[:n_w], refs[n_w : n_w + 2], refs[n_w + 2 : n_w + 8], refs[n_w + 8]
    x_mem, w_mem, acc, x_sem, w_sem = refs[n_w + 9 :]
    x_lo, z = cand_ref[5], cand_ref[6]
    slots, blk, both = w_mem.shape
    share, width = blk // z_count, both // 2
    w_copies = []
    for k in range(slots):
        mine = []
        for i, ref in enumerate(w_refs):
            if i < z_count - 1:
                origin, sides = (z - (i + 1) // 2 if i % 2 else z + i // 2), (0, 1)
            else:
                origin, sides = z + z_count // 2, (i - z_count + 1,)
            at = pl.ds(pl.multiple_of((origin + z_count) % z_count * share, 16), share)
            for n, side in enumerate(sides):
                there = w_mem.at[k, at, pl.ds(side * width, width)]
                mine.append(pltpu.make_async_copy(ref.at[n, k], there, w_sem.at[k, i, n]))
        w_copies.append(mine)
    x_copies = []
    for m in range(2):
        at = pl.ds(m * rows, rows)
        for j in range(2):
            col = pl.multiple_of((x_lo ^ j) * blk, blk)
            x_copies.append(pltpu.make_async_copy(s_refs[m].at[:, pl.ds(col, blk)], x_mem.at[j, at], x_sem.at[m, j]))
        for d in range(3):
            x_copies.append(pltpu.make_async_copy(p_refs[d * 2 + m], x_mem.at[2 + d, at], x_sem.at[m, 2 + d]))
    for copy in w_copies[0] + x_copies:
        copy.start()
    for mine in w_copies[1:]:
        for copy in mine:
            copy.start()
    for copy in x_copies:
        copy.wait()
    for k in range(slots):
        for copy in w_copies[k]:
            copy.wait()
        term = jnp.dot(x_mem[cand_ref[k]], w_mem[k], preferred_element_type=jnp.float32)
        g, u = term[:, :width] * gs_ref[k], term[:, width:] * us_ref[k]
        if k == 0:
            acc[:, :width] = g
            acc[:, width:] = u
        else:
            acc[:, :width] += g
            acc[:, width:] += u
    g = acc[:, :width]
    out = (g / (1.0 + jnp.exp(-g)) * acc[:, width:]).astype(jnp.bfloat16)
    out_ref[0] = out[:rows]
    out_ref[1] = out[rows:]


def gate_up(cand, gs, us, weights, own_rows, partner_rows):
    rows, features = own_rows[0].shape
    blk = features // 2
    _, slots, share, width = weights[0].shape
    z_count = blk // share
    flops = 2 * 2 * 2 * rows * slots * blk * width
    return pl.pallas_call(
        functools.partial(gate_up_kernel, rows=rows, z_count=z_count),
        out_shape=jax.ShapeDtypeStruct((2, rows, width), jnp.bfloat16),
        in_specs=[SMEM] * 3 + [HBM] * (len(weights) + 8),
        out_specs=VMEM,
        scratch_shapes=[
            pltpu.VMEM((slots, 2 * rows, blk), jnp.bfloat16),
            pltpu.VMEM((slots, blk, 2 * width), jnp.bfloat16),
            pltpu.VMEM((2 * rows, 2 * width), jnp.float32),
            pltpu.SemaphoreType.DMA((2, 5)),
            pltpu.SemaphoreType.DMA((slots, z_count + 1, 2)),
        ],
        compiler_params=pltpu.CompilerParams(vmem_limit_bytes=VMEM_BYTES),
        cost_estimate=pl.CostEstimate(flops=flops, bytes_accessed=10 * 2**20, transcendentals=2 * rows * width),
    )(cand, gs, us, *weights, *own_rows, *partner_rows)


def latent_kernel(own_ref, lin_ref, *refs):
    pieces, hidden_ref, part_ref = refs[:4], refs[4], refs[5]
    width = pieces[0].shape[1]
    total = None
    for m in range(4):
        at = pl.ds(pl.multiple_of((own_ref[0] ^ m) * width, width), width)
        piece = pieces[m][...]
        hidden_ref[:, at] = piece
        term = jnp.dot(piece, lin_ref[at], preferred_element_type=jnp.float32)
        total = term if total is None else total + term
    part_ref[...] = total.astype(jnp.bfloat16)


def per_device(tokens, gate_weight, up_weight, gate_scale, up_scale, partners, latent_in, latent_out):
    rows, features = tokens.shape
    blocks, slots, share, blk = gate_weight.shape
    feat_count = lax.axis_size("feat")
    half = blk // 2
    feat, tok = lax.axis_index("feat"), lax.axis_index("tok")
    member, z = tok % GROUP, tok // GROUP
    x_lo, core = member // 2, member % 2
    block_id = feat * blocks + x_lo

    own = member[None].astype(jnp.int32)
    packed = pl.pallas_call(
        pack_kernel,
        out_shape=[jax.ShapeDtypeStruct((2, slots, share, half), jnp.bfloat16)] * 4,
        in_specs=[SMEM, VMEM, VMEM],
        out_specs=[VMEM] * 4,
    )(own, gate_weight, up_weight)

    def place(got):
        shape = got[0].shape
        out = pl.pallas_call(
            place_kernel,
            out_shape=jax.ShapeDtypeStruct(shape[:2] + (4,) + shape[2:], jnp.bfloat16),
            in_specs=[SMEM] + [VMEM] * 4,
            out_specs=VMEM,
        )(own, *got)
        return out.reshape(shape[:2] + (4 * shape[2],) + shape[3:])

    def block_of(value):
        return lax.dynamic_slice(value, (0, x_lo * blk), (rows, blk))

    def step(forward, back):
        return shifted(forward, 1), shifted(back, -1)

    far = [swapped(packed[m], "tok", m) for m in (2, 3)]
    near = swapped(packed[1], "tok", 1)
    w0 = place([packed[0], near, *far])
    barrier = lax.optimization_barrier
    first = block_of(tokens)
    p0_y1, p0_y2 = swapped(first, "feat", 2), swapped(first, "feat", 4)
    w0, later = barrier((w0, tokens))
    w1 = step(w0, w0)
    s2 = swapped(later, "tok", 2)
    first, p0_y1, p0_y2 = barrier((first, p0_y1, p0_y2))
    p0 = [swapped(first, "feat", 1), p0_y1, p0_y2]
    w1, s2, p0, later = barrier((w1, s2, p0, later))
    w2 = step(*w1)
    second = block_of(s2)
    p2 = [swapped(second, "feat", mask) for mask in (1, 2, 4)]
    w2, p2, p0, s2, later = barrier((w2, p2, p0, s2, later))
    w3 = step(*w2)
    s3 = swapped(s2, "tok", 1)
    p3 = [swapped(v, "tok", 1) for v in p2]
    w3, s3, p3, p0, later = barrier((w3, s3, p3, p0, later))
    w4 = step(w3[0][:1], w3[1][1:])
    s1 = swapped(later, "tok", 1)
    p1 = [swapped(v, "tok", 1) for v in p0]
    full = (w0, *w1, *w2, *w3, *w4)

    wanted = lax.dynamic_index_in_dim(partners, block_id, 0, keepdims=False)
    labels = block_id ^ jnp.array([0, 1, 2, 4, 8], jnp.int32)
    order = jnp.sum(jnp.where(wanted[:, None] == labels[None, :], jnp.arange(5, dtype=jnp.int32)[None, :], 0), axis=1)
    cand = jnp.concatenate([order, jnp.stack([x_lo, z]).astype(jnp.int32)])
    gs = lax.dynamic_index_in_dim(gate_scale, x_lo, 0, keepdims=False)
    us = lax.dynamic_index_in_dim(up_scale, x_lo, 0, keepdims=False)

    made = gate_up(cand, gs, us, full, [s2, s3], [p[d] for d in range(3) for p in (p2, p3)])
    hidden2, hidden3 = swapped(made[0], "tok", 2), swapped(made[1], "tok", 3)
    made = gate_up(cand, gs, us, full, [tokens, s1], [p[d] for d in range(3) for p in (p0, p1)])
    hidden_pieces = [made[0], swapped(made[1], "tok", 1), hidden2, hidden3]
    hidden, part = pl.pallas_call(
        latent_kernel,
        out_shape=(
            jax.ShapeDtypeStruct((rows, features), jnp.bfloat16),
            jax.ShapeDtypeStruct((rows, latent_in.shape[1]), jnp.bfloat16),
        ),
        in_specs=[SMEM] + [VMEM] * 5,
        out_specs=(VMEM, VMEM),
        compiler_params=pltpu.CompilerParams(vmem_limit_bytes=VMEM_BYTES),
        cost_estimate=pl.CostEstimate(flops=2 * rows * features * latent_in.shape[1], bytes_accessed=4 * 2**20, transcendentals=0),
    )(own, latent_in, *hidden_pieces)

    parts = part.reshape(feat_count, rows // feat_count, -1)
    terms = lax.all_to_all(parts, "feat", 0, 0)
    mine = jnp.sum(terms.astype(jnp.float32), axis=0).astype(jnp.bfloat16)
    latent = lax.all_to_all(jnp.broadcast_to(mine[None], parts.shape), "feat", 0, 0).reshape(rows, -1)
    rank_term = jnp.dot(latent, latent_out, preferred_element_type=jnp.float32).astype(jnp.bfloat16)
    return hidden, rank_term


def solution(mesh):
    placed = (
        P("tok", "feat"),
        P("feat", None, "tok", None),
        P("feat", None, "tok", None),
        P("feat", None),
        P("feat", None),
        P(),
        P("feat", None),
        P(None, "feat"),
    )
    return jax.shard_map(
        per_device,
        mesh=mesh,
        in_specs=placed,
        out_specs=(P("tok", "feat"), P("tok", "feat")),
        check_vma=False,
    )
```

```python
import functools
import jax
import jax.numpy as jnp
from jax import lax
from jax.experimental import pallas as pl
from jax.experimental.pallas import tpu as pltpu
from jax.sharding import PartitionSpec as P

GROUP = 4
HBM = pl.BlockSpec(memory_space=pltpu.HBM)
SMEM = pl.BlockSpec(memory_space=pltpu.SMEM)
VMEM = pl.BlockSpec(memory_space=pltpu.VMEM)
VMEM_BYTES = 60 * 2**20
SMALL_BYTES = 16 * 2**20
ANY = pl.BlockSpec(memory_space=pl.ANY)


def swapped(value, axis, mask):
    return lax.ppermute(value, axis, [(i, i ^ mask) for i in range(lax.axis_size(axis))])


def shifted(value, step):
    count = lax.axis_size("tok")
    return lax.ppermute(value, "tok", [(i, (i + step * GROUP) % count) for i in range(count)])


def pack_kernel(own_ref, gate_ref, up_ref, *out_refs):
    half = gate_ref.shape[3] // 2
    for m in range(4):
        to = own_ref[0] ^ m
        at = pl.ds(pl.multiple_of(to % 2 * half, 128), half)
        for side, ref in enumerate((gate_ref, up_ref)):
            out_refs[m][side] = ref[to // 2, :, :, at]


def place_kernel(own_ref, *refs):
    for m in range(4):
        refs[4][:, :, own_ref[0] ^ m] = refs[m][...]


def halves_kernel(f_ref, b_ref, f_out, b_out, sem):
    copies = [
        pltpu.make_async_copy(f_ref.at[pl.ds(0, 1)], f_out, sem.at[0]),
        pltpu.make_async_copy(b_ref.at[pl.ds(1, 1)], b_out, sem.at[1]),
    ]
    for copy in copies:
        copy.start()
    for copy in copies:
        copy.wait()


def join_kernel(*refs):
    t_ref, s_ref, x_ref, *y_refs = refs[:7]
    own_out, partner_out, sem = refs[7:]
    rows = t_ref.shape[0]
    pairs = [(t_ref, own_out.at[pl.ds(0, rows)]), (s_ref, own_out.at[pl.ds(rows, rows)]), (x_ref, partner_out.at[0])]
    for i, y_ref in enumerate(y_refs):
        pairs.append((y_ref, partner_out.at[1 + i // 2, pl.ds(i % 2 * rows, rows)]))
    copies = [pltpu.make_async_copy(source, there, sem.at[i]) for i, (source, there) in enumerate(pairs)]
    for copy in copies:
        copy.start()
    for copy in copies:
        copy.wait()


def token_copies(own_refs, partner_refs, x_mem, x_sem, x_lo, first, rows, start, width):
    blk = partner_refs[0].shape[2]
    copies = []
    for j in range(5):
        mine = []
        for core in range(2):
            if j < 2:
                column = pl.multiple_of((x_lo ^ j) * blk + start, 128)
                source = own_refs[core].at[pl.ds(first, rows), pl.ds(column, width)]
            else:
                column = pl.multiple_of(start, 128)
                source = partner_refs[core].at[j - 2, pl.ds(first, rows), pl.ds(column, width)]
            mine.append(pltpu.make_async_copy(source, x_mem.at[j, pl.ds(core * rows, rows)], x_sem.at[core, j]))
        copies.append(mine)
    return copies


def early_kernel(place_ref, gs_ref, us_ref, *refs, z_count):
    n_w = z_count - 1
    w_refs, own_refs, partner_refs, acc = refs[:n_w], refs[n_w : n_w + 2], refs[n_w + 2 : n_w + 4], refs[n_w + 4]
    x_mem, w_mem, x_sem, w_sem = refs[n_w + 5 :]
    x_lo, z = place_ref[5], place_ref[6]
    _, blk, both = w_mem.shape
    share, width = blk // z_count, both // 2
    copies = token_copies(own_refs, partner_refs, x_mem, x_sem, x_lo, 0, own_refs[0].shape[0], 0, blk)
    for j in range(5):
        for i, ref in enumerate(w_refs):
            origin = z - (i + 1) // 2 if i % 2 else z + i // 2
            at = pl.ds(pl.multiple_of((origin + z_count) % z_count * share, 16), share)
            for side in range(2):
                there = w_mem.at[j, at, pl.ds(side * width, width)]
                copies[j].append(pltpu.make_async_copy(ref.at[side, place_ref[j]], there, w_sem.at[j, i, side]))
        for copy in copies[j]:
            copy.start()
    last = pl.ds(pl.multiple_of((z + z_count // 2) % z_count * share, 16), share)
    for j in range(5):
        w_mem[j, last] = jnp.zeros((share, both), w_mem.dtype)
    for j in range(5):
        for copy in copies[j]:
            copy.wait()
        term = jnp.dot(x_mem[j], w_mem[j], preferred_element_type=jnp.float32)
        g, u = term[:, :width] * gs_ref[place_ref[j]], term[:, width:] * us_ref[place_ref[j]]
        if j == 0:
            acc[:, :width] = g
            acc[:, width:] = u
        else:
            acc[:, :width] += g
            acc[:, width:] += u


def early(place, gs, us, weights, own_rows, partner_rows):
    rows, features = own_rows[0].shape
    rows //= 2
    blk = features // 2
    _, slots, share, width = weights[0].shape
    z_count = blk // share
    return pl.pallas_call(
        functools.partial(early_kernel, z_count=z_count),
        out_shape=jax.ShapeDtypeStruct((4 * rows, 2 * width), jnp.float32),
        in_specs=[SMEM] * 3 + [HBM] * (len(weights) + 4),
        out_specs=VMEM,
        scratch_shapes=[
            pltpu.VMEM((slots, 4 * rows, blk), jnp.bfloat16),
            pltpu.VMEM((slots, blk, 2 * width), jnp.bfloat16),
            pltpu.SemaphoreType.DMA((2, slots)),
            pltpu.SemaphoreType.DMA((slots, z_count - 1, 2)),
        ],
        compiler_params=pltpu.CompilerParams(vmem_limit_bytes=VMEM_BYTES),
        cost_estimate=pl.CostEstimate(
            flops=2 * 2 * 4 * rows * slots * blk * width, bytes_accessed=17 * 2**20, transcendentals=0
        ),
    )(place, gs, us, *weights, *own_rows, *partner_rows)


def late_kernel(place_ref, gs_ref, us_ref, *refs, z_count, window, first):
    w_refs, acc_ref, own_refs, partner_refs, out_refs = refs[:2], refs[2], refs[3:5], refs[5:7], refs[7:9]
    x_mem, w_mem, acc, x_sem, w_sem, acc_sem = refs[9:]
    x_lo, z = place_ref[5], place_ref[6]
    share, width = w_refs[0].shape[2:]
    rows, blk = own_refs[0].shape[0] // 2, own_refs[0].shape[1] // 2
    row = (z + z_count // 2) % z_count * share
    start = jnp.minimum(row // 128 * 128, blk - window)
    at = pl.ds(pl.multiple_of(row - start, 16), share)
    acc_copies = [
        pltpu.make_async_copy(
            acc_ref.at[pl.ds((2 * core + first) * rows, rows)], acc.at[pl.ds(core * rows, rows)], acc_sem.at[core]
        )
        for core in range(2)
    ]
    copies = token_copies(own_refs, partner_refs, x_mem, x_sem, x_lo, first * rows, rows, start, window)
    for mine in copies:
        for copy in mine:
            copy.start()
    for copy in acc_copies:
        copy.start()
    w_mem[...] = jnp.zeros_like(w_mem)
    w_copies = []
    for j in range(5):
        w_copies.append([])
        for side in range(2):
            there = w_mem.at[j, at, pl.ds(side * width, width)]
            w_copies[j].append(pltpu.make_async_copy(w_refs[side].at[0, place_ref[j]], there, w_sem.at[j, side]))
            w_copies[j][side].start()
    for copy in acc_copies:
        copy.wait()
    for j in range(5):
        for copy in copies[j] + w_copies[j]:
            copy.wait()
        term = jnp.dot(x_mem[j], w_mem[j], preferred_element_type=jnp.float32)
        acc[:, :width] += term[:, :width] * gs_ref[place_ref[j]]
        acc[:, width:] += term[:, width:] * us_ref[place_ref[j]]
    g = acc[:, :width]
    out = (g / (1.0 + jnp.exp(-g)) * acc[:, width:]).astype(jnp.bfloat16)
    out_refs[0][...] = out[:rows]
    out_refs[1][...] = out[rows:]


def late(place, gs, us, weights, acc, own_rows, partner_rows, first):
    rows, features = own_rows[0].shape
    rows //= 2
    blk = features // 2
    _, slots, share, width = weights[0].shape
    window = min(2 * 128 * ((share + 127) // 128), blk)
    return pl.pallas_call(
        functools.partial(late_kernel, z_count=blk // share, window=window, first=first),
        out_shape=[jax.ShapeDtypeStruct((rows, width), jnp.bfloat16)] * 2,
        in_specs=[SMEM] * 3 + [HBM] * 7,
        out_specs=[VMEM] * 2,
        scratch_shapes=[
            pltpu.VMEM((slots, 2 * rows, window), jnp.bfloat16),
            pltpu.VMEM((slots, window, 2 * width), jnp.bfloat16),
            pltpu.VMEM((2 * rows, 2 * width), jnp.float32),
            pltpu.SemaphoreType.DMA((2, slots)),
            pltpu.SemaphoreType.DMA((slots, 2)),
            pltpu.SemaphoreType.DMA((2,)),
        ],
        compiler_params=pltpu.CompilerParams(vmem_limit_bytes=VMEM_BYTES),
        cost_estimate=pl.CostEstimate(
            flops=2 * 2 * 2 * rows * slots * window * width, bytes_accessed=4 * 2**20, transcendentals=2 * rows * width
        ),
    )(place, gs, us, *weights, acc, *own_rows, *partner_rows)


def latent_kernel(own_ref, lin_ref, *refs):
    pieces, hidden_ref, part_ref = refs[:4], refs[4], refs[5]
    width = pieces[0].shape[1]
    total = None
    for m in range(4):
        at = pl.ds(pl.multiple_of((own_ref[0] ^ m) * width, width), width)
        piece = pieces[m][...]
        hidden_ref[:, at] = piece
        term = jnp.dot(piece, lin_ref[at], preferred_element_type=jnp.float32)
        total = term if total is None else total + term
    part_ref[...] = total.astype(jnp.bfloat16)


def per_device(tokens, gate_weight, up_weight, gate_scale, up_scale, partners, latent_in, latent_out):
    rows, features = tokens.shape
    blocks, slots, share, blk = gate_weight.shape
    feat_count = lax.axis_size("feat")
    half = blk // 2
    feat, tok = lax.axis_index("feat"), lax.axis_index("tok")
    member, z = tok % GROUP, tok // GROUP
    x_lo, core = member // 2, member % 2
    block_id = feat * blocks + x_lo

    own = member[None].astype(jnp.int32)
    packed = pl.pallas_call(
        pack_kernel,
        out_shape=[jax.ShapeDtypeStruct((2, slots, share, half), jnp.bfloat16)] * 4,
        in_specs=[SMEM, VMEM, VMEM],
        out_specs=[VMEM] * 4,
        compiler_params=pltpu.CompilerParams(vmem_limit_bytes=SMALL_BYTES),
    )(own, gate_weight, up_weight)

    def place(got):
        shape = got[0].shape
        out = pl.pallas_call(
            place_kernel,
            out_shape=jax.ShapeDtypeStruct(shape[:2] + (4,) + shape[2:], jnp.bfloat16),
            in_specs=[SMEM] + [VMEM] * 4,
            out_specs=VMEM,
            compiler_params=pltpu.CompilerParams(vmem_limit_bytes=SMALL_BYTES),
        )(own, *got)
        return out.reshape(shape[:2] + (4 * shape[2],) + shape[3:])

    def block_of(value):
        return lax.dynamic_slice(value, (0, x_lo * blk), (rows, blk))

    def step(forward, back):
        return shifted(forward, 1), shifted(back, -1)

    far = [swapped(packed[m], "tok", m) for m in (2, 3)]
    near = swapped(packed[1], "tok", 1)
    w0 = place([packed[0], near, *far])
    barrier = lax.optimization_barrier
    first = block_of(tokens)
    p0_y1, p0_y2 = swapped(first, "feat", 2), swapped(first, "feat", 4)
    w0, later = barrier((w0, tokens))
    w1 = step(w0, w0)
    s2 = swapped(later, "tok", 2)
    w1, s2, p0_y1, p0_y2, first, later = barrier((w1, s2, p0_y1, p0_y2, first, later))
    w2 = step(*w1)
    second = block_of(s2)
    p_x = swapped(jnp.concatenate([first, second]), "feat", 1)
    p2_y1, p2_y2 = swapped(second, "feat", 2), swapped(second, "feat", 4)
    w2, p_x, p2_y1, p2_y2, p0_y1, p0_y2, s2, later = barrier((w2, p_x, p2_y1, p2_y2, p0_y1, p0_y2, s2, later))
    w3 = step(*w2)
    own0, partner0 = pl.pallas_call(
        join_kernel,
        out_shape=[
            jax.ShapeDtypeStruct((2 * rows, features), jnp.bfloat16),
            jax.ShapeDtypeStruct((3, 2 * rows, blk), jnp.bfloat16),
        ],
        in_specs=[HBM] * 7,
        out_specs=[HBM] * 2,
        scratch_shapes=[pltpu.SemaphoreType.DMA((7,))],
    )(later, s2, p_x, p0_y1, p2_y1, p0_y2, p2_y2)
    own1, partner1 = swapped(own0, "tok", 1), swapped(partner0, "tok", 1)
    w3, own0, own1, partner0, partner1 = barrier((w3, own0, own1, partner0, partner1))
    cut = pl.pallas_call(
        halves_kernel,
        out_shape=[jax.ShapeDtypeStruct((1,) + w3[0].shape[1:], jnp.bfloat16)] * 2,
        in_specs=[ANY] * 2,
        out_specs=[ANY] * 2,
        scratch_shapes=[pltpu.SemaphoreType.DMA((2,))],
        compiler_params=pltpu.CompilerParams(vmem_limit_bytes=SMALL_BYTES),
    )(*w3)
    w4 = step(*cut)

    wanted = lax.dynamic_index_in_dim(partners, block_id, 0, keepdims=False)
    labels = block_id ^ jnp.array([0, 1, 2, 4, 8], jnp.int32)
    order = jnp.sum(jnp.where(labels[:, None] == wanted[None, :], jnp.arange(5, dtype=jnp.int32)[None, :], 0), axis=1)
    here = jnp.concatenate([order, jnp.stack([x_lo, z]).astype(jnp.int32)])
    gs = lax.dynamic_index_in_dim(gate_scale, x_lo, 0, keepdims=False)
    us = lax.dynamic_index_in_dim(up_scale, x_lo, 0, keepdims=False)

    sides = (own0, own1), (partner0, partner1)
    acc = early(here, gs, us, (w0, *w1, *w2, *w3), *sides)
    far_hidden = [swapped(v, "tok", mask) for v, mask in zip(late(here, gs, us, w4, acc, *sides, 1), (2, 3))]
    made = late(here, gs, us, w4, acc, *sides, 0)
    hidden_pieces = [made[0], swapped(made[1], "tok", 1), *far_hidden]
    hidden, part = pl.pallas_call(
        latent_kernel,
        out_shape=(
            jax.ShapeDtypeStruct((rows, features), jnp.bfloat16),
            jax.ShapeDtypeStruct((rows, latent_in.shape[1]), jnp.bfloat16),
        ),
        in_specs=[SMEM] + [VMEM] * 5,
        out_specs=(VMEM, VMEM),
        compiler_params=pltpu.CompilerParams(vmem_limit_bytes=SMALL_BYTES),
        cost_estimate=pl.CostEstimate(flops=2 * rows * features * latent_in.shape[1], bytes_accessed=4 * 2**20, transcendentals=0),
    )(own, latent_in, *hidden_pieces)

    parts = part.reshape(feat_count, rows // feat_count, -1)
    terms = lax.all_to_all(parts, "feat", 0, 0)
    mine = jnp.sum(terms.astype(jnp.float32), axis=0).astype(jnp.bfloat16)
    latent = lax.all_to_all(jnp.broadcast_to(mine[None], parts.shape), "feat", 0, 0).reshape(rows, -1)
    rank_term = jnp.dot(latent, latent_out, preferred_element_type=jnp.float32).astype(jnp.bfloat16)
    return hidden, rank_term


def solution(mesh):
    placed = (
        P("tok", "feat"),
        P("feat", None, "tok", None),
        P("feat", None, "tok", None),
        P("feat", None),
        P("feat", None),
        P(),
        P("feat", None),
        P(None, "feat"),
    )
    return jax.shard_map(
        per_device,
        mesh=mesh,
        in_specs=placed,
        out_specs=(P("tok", "feat"), P("tok", "feat")),
        check_vma=False,
    )
```

```python
import functools
import jax
import jax.numpy as jnp
from jax import lax
from jax.experimental import pallas as pl
from jax.experimental.pallas import tpu as pltpu
from jax.sharding import PartitionSpec as P

GROUP = 4
SMEM = pl.BlockSpec(memory_space=pltpu.SMEM)
VMEM = pl.BlockSpec(memory_space=pltpu.VMEM)
VMEM_BYTES = 30 * 2**20
SMALL_BYTES = 16 * 2**20


def swapped(value, axis, mask):
    return lax.ppermute(value, axis, [(i, i ^ mask) for i in range(lax.axis_size(axis))])


def shifted(value, step):
    count = lax.axis_size("tok")
    return lax.ppermute(value, "tok", [(i, (i + step * GROUP) % count) for i in range(count)])


def pack_kernel(own_ref, gate_ref, up_ref, *out_refs):
    half = gate_ref.shape[3] // 2
    for m in range(4):
        to = own_ref[0] ^ m
        at = pl.ds(pl.multiple_of(to % 2 * half, 128), half)
        for side, ref in enumerate((gate_ref, up_ref)):
            out_refs[m][side] = ref[to // 2, :, :, at]


def place_kernel(own_ref, *refs):
    for m in range(4):
        refs[4][:, :, own_ref[0] ^ m] = refs[m][...]


def halves_kernel(f_ref, b_ref, f_out, b_out):
    f_out[...] = f_ref[...]
    b_out[...] = b_ref[...]


def block_of_rows(own_refs, partner_refs, j, x_lo, rows, start, width):
    blk = partner_refs[0].shape[2]
    if j < 2:
        column = pl.ds(pl.multiple_of((x_lo ^ j) * blk + start, 128), width)
        return jnp.concatenate([ref[rows, column] for ref in own_refs])
    column = pl.ds(pl.multiple_of(start, 128), width)
    return jnp.concatenate([ref[j - 2, rows, column] for ref in partner_refs])


def last_window(z, z_count, share, blk, window):
    row = (z + z_count // 2) % z_count * share
    return row, jnp.minimum(row // 128 * 128, blk - window)


def early_kernel(place_ref, gs_ref, us_ref, *refs, z_count, window):
    n_w = z_count - 1
    w_refs, own_refs, partner_refs = refs[:n_w], refs[n_w : n_w + 2], refs[n_w + 2 : n_w + 4]
    acc, windows, w_mem = refs[n_w + 4 :]
    x_lo, z = place_ref[5], place_ref[6]
    blk, both = w_mem.shape[1:]
    share, width = blk // z_count, both // 2
    row, start = last_window(z, z_count, share, blk, window)
    last = pl.ds(pl.multiple_of(row, 16), share)
    for j in range(5):
        slot = place_ref[j]
        w_mem[j % 2, last] = jnp.zeros((share, both), w_mem.dtype)
        for i, ref in enumerate(w_refs):
            origin = z - (i + 1) // 2 if i % 2 else z + i // 2
            at = pl.ds(pl.multiple_of((origin + z_count) % z_count * share, 16), share)
            for side in range(2):
                w_mem[j % 2, at, side * width : (side + 1) * width] = ref[side, slot]
        windows[j] = block_of_rows(own_refs, partner_refs, j, x_lo, slice(None), start, window)
        x = block_of_rows(own_refs, partner_refs, j, x_lo, slice(None), 0, blk)
        term = jnp.dot(x, w_mem[j % 2], preferred_element_type=jnp.float32)
        g, u = term[:, :width] * gs_ref[slot], term[:, width:] * us_ref[slot]
        if j == 0:
            acc[:, :width] = g
            acc[:, width:] = u
        else:
            acc[:, :width] += g
            acc[:, width:] += u


def early(place, gs, us, weights, own_rows, partner_rows):
    blk = own_rows[0].shape[1] // 2
    rows = 2 * own_rows[0].shape[0]
    _, slots, share, width = weights[0].shape
    window = min(2 * 128 * ((share + 127) // 128), blk)
    return pl.pallas_call(
        functools.partial(early_kernel, z_count=blk // share, window=window),
        out_shape=[
            jax.ShapeDtypeStruct((rows, 2 * width), jnp.float32),
            jax.ShapeDtypeStruct((slots, rows, window), jnp.bfloat16),
        ],
        in_specs=[SMEM] * 3 + [VMEM] * (len(weights) + 4),
        out_specs=[VMEM] * 2,
        scratch_shapes=[pltpu.VMEM((2, blk, 2 * width), jnp.bfloat16)],
        compiler_params=pltpu.CompilerParams(vmem_limit_bytes=VMEM_BYTES),
        cost_estimate=pl.CostEstimate(flops=2**20, bytes_accessed=2**20, transcendentals=0),
    )(place, gs, us, *weights, *own_rows, *partner_rows)


def late_kernel(place_ref, gs_ref, us_ref, *refs, z_count, first):
    w_refs, acc_ref, window_ref, out_refs = refs[:2], refs[2], refs[3], refs[4:6]
    w_mem, acc = refs[6:]
    z = place_ref[6]
    share, width = w_refs[0].shape[2:]
    slots, rows, window = window_ref.shape
    rows //= 4
    row, start = last_window(z, z_count, share, z_count * share, window)
    at = pl.ds(pl.multiple_of(row - start, 16), share)
    w_mem[...] = jnp.zeros_like(w_mem)
    mine = [pl.ds((2 * core + first) * rows, rows) for core in range(2)]
    for core in range(2):
        acc[pl.ds(core * rows, rows)] = acc_ref[mine[core]]
    for j in range(slots):
        slot = place_ref[j]
        for side in range(2):
            w_mem[j, at, side * width : (side + 1) * width] = w_refs[side][0, slot]
        x = jnp.concatenate([window_ref[j, at_core] for at_core in mine])
        term = jnp.dot(x, w_mem[j], preferred_element_type=jnp.float32)
        acc[:, :width] += term[:, :width] * gs_ref[slot]
        acc[:, width:] += term[:, width:] * us_ref[slot]
    g = acc[:, :width]
    out = (g / (1.0 + jnp.exp(-g)) * acc[:, width:]).astype(jnp.bfloat16)
    out_refs[0][...] = out[:rows]
    out_refs[1][...] = out[rows:]


def late(place, gs, us, weights, acc, windows, z_count, first):
    slots, rows, window = windows.shape
    rows //= 4
    width = weights[0].shape[3]
    return pl.pallas_call(
        functools.partial(late_kernel, z_count=z_count, first=first),
        out_shape=[jax.ShapeDtypeStruct((rows, width), jnp.bfloat16)] * 2,
        in_specs=[SMEM] * 3 + [VMEM] * 4,
        out_specs=[VMEM] * 2,
        scratch_shapes=[
            pltpu.VMEM((slots, window, 2 * width), jnp.bfloat16),
            pltpu.VMEM((2 * rows, 2 * width), jnp.float32),
        ],
        compiler_params=pltpu.CompilerParams(vmem_limit_bytes=SMALL_BYTES),
        cost_estimate=pl.CostEstimate(
            flops=2 * 2 * 2 * rows * slots * window * width, bytes_accessed=4 * 2**20, transcendentals=2 * rows * width
        ),
    )(place, gs, us, *weights, acc, windows)


def latent_kernel(own_ref, lin_ref, *refs):
    pieces, hidden_ref, part_ref = refs[:4], refs[4], refs[5]
    width = pieces[0].shape[1]
    total = None
    for m in range(4):
        at = pl.ds(pl.multiple_of((own_ref[0] ^ m) * width, width), width)
        piece = pieces[m][...]
        hidden_ref[:, at] = piece
        term = jnp.dot(piece, lin_ref[at], preferred_element_type=jnp.float32)
        total = term if total is None else total + term
    part_ref[...] = total.astype(jnp.bfloat16)


def per_device(tokens, gate_weight, up_weight, gate_scale, up_scale, partners, latent_in, latent_out):
    rows, features = tokens.shape
    blocks, slots, share, blk = gate_weight.shape
    feat_count = lax.axis_size("feat")
    half = blk // 2
    feat, tok = lax.axis_index("feat"), lax.axis_index("tok")
    member, z = tok % GROUP, tok // GROUP
    x_lo, core = member // 2, member % 2
    block_id = feat * blocks + x_lo

    own = member[None].astype(jnp.int32)
    packed = pl.pallas_call(
        pack_kernel,
        out_shape=[jax.ShapeDtypeStruct((2, slots, share, half), jnp.bfloat16)] * 4,
        in_specs=[SMEM, VMEM, VMEM],
        out_specs=[VMEM] * 4,
        compiler_params=pltpu.CompilerParams(vmem_limit_bytes=SMALL_BYTES),
    )(own, gate_weight, up_weight)

    def place(got):
        shape = got[0].shape
        out = pl.pallas_call(
            place_kernel,
            out_shape=jax.ShapeDtypeStruct(shape[:2] + (4,) + shape[2:], jnp.bfloat16),
            in_specs=[SMEM] + [VMEM] * 4,
            out_specs=VMEM,
            compiler_params=pltpu.CompilerParams(vmem_limit_bytes=SMALL_BYTES),
        )(own, *got)
        return out.reshape(shape[:2] + (4 * shape[2],) + shape[3:])

    def block_of(value):
        return lax.dynamic_slice(value, (0, x_lo * blk), (rows, blk))

    def step(forward, back):
        return shifted(forward, 1), shifted(back, -1)

    far = [swapped(packed[m], "tok", m) for m in (2, 3)]
    near = swapped(packed[1], "tok", 1)
    w0 = place([packed[0], near, *far])
    barrier = lax.optimization_barrier
    first = block_of(tokens)
    p0_y1, p0_y2 = swapped(first, "feat", 2), swapped(first, "feat", 4)
    w0, later = barrier((w0, tokens))
    w1 = step(w0, w0)
    s2 = swapped(later, "tok", 2)
    w1, s2, first, later = barrier((w1, s2, first, later))
    w2 = step(*w1)
    second = block_of(s2)
    p_x = swapped(jnp.concatenate([first, second]), "feat", 1)
    second, p0_y1, p0_y2 = barrier((second, p0_y1, p0_y2))
    p2_y1, p2_y2 = swapped(second, "feat", 2), swapped(second, "feat", 4)
    w2, p_x, p2_y1, p2_y2, p0_y1, p0_y2, s2, later = barrier((w2, p_x, p2_y1, p2_y2, p0_y1, p0_y2, s2, later))
    w3 = step(*w2)
    own0 = jnp.concatenate([later, s2])
    partner0 = jnp.stack([p_x, jnp.concatenate([p0_y1, p2_y1]), jnp.concatenate([p0_y2, p2_y2])])
    own1, partner1 = swapped(own0, "tok", 1), swapped(partner0, "tok", 1)
    w3, own0, own1, partner0, partner1 = barrier((w3, own0, own1, partner0, partner1))
    half_shape = (1,) + w3[0].shape[1:]
    cut = pl.pallas_call(
        halves_kernel,
        grid=(1,),
        out_shape=[jax.ShapeDtypeStruct(half_shape, jnp.bfloat16)] * 2,
        in_specs=[pl.BlockSpec(half_shape, lambda i: (0, 0, 0, 0)), pl.BlockSpec(half_shape, lambda i: (1, 0, 0, 0))],
        out_specs=[pl.BlockSpec(half_shape, lambda i: (0, 0, 0, 0))] * 2,
        compiler_params=pltpu.CompilerParams(vmem_limit_bytes=SMALL_BYTES),
    )(*w3)
    w4 = step(*cut)

    wanted = lax.dynamic_index_in_dim(partners, block_id, 0, keepdims=False)
    labels = block_id ^ jnp.array([0, 1, 2, 4, 8], jnp.int32)
    order = jnp.sum(jnp.where(labels[:, None] == wanted[None, :], jnp.arange(5, dtype=jnp.int32)[None, :], 0), axis=1)
    here = jnp.concatenate([order, jnp.stack([x_lo, z]).astype(jnp.int32)])
    gs = lax.dynamic_index_in_dim(gate_scale, x_lo, 0, keepdims=False)
    us = lax.dynamic_index_in_dim(up_scale, x_lo, 0, keepdims=False)

    acc, windows = early(here, gs, us, (w0, *w1, *w2, *w3), (own0, own1), (partner0, partner1))
    z_count = lax.axis_size("tok") // GROUP
    made = late(here, gs, us, w4, acc, windows, z_count, 1)
    far_hidden = [swapped(v, "tok", mask) for v, mask in zip(made, (2, 3))]
    made = late(here, gs, us, w4, acc, windows, z_count, 0)
    hidden_pieces = [made[0], swapped(made[1], "tok", 1), *far_hidden]
    hidden, part = pl.pallas_call(
        latent_kernel,
        out_shape=(
            jax.ShapeDtypeStruct((rows, features), jnp.bfloat16),
            jax.ShapeDtypeStruct((rows, latent_in.shape[1]), jnp.bfloat16),
        ),
        in_specs=[SMEM] + [VMEM] * 5,
        out_specs=(VMEM, VMEM),
        compiler_params=pltpu.CompilerParams(vmem_limit_bytes=SMALL_BYTES),
        cost_estimate=pl.CostEstimate(flops=2 * rows * features * latent_in.shape[1], bytes_accessed=4 * 2**20, transcendentals=0),
    )(own, latent_in, *hidden_pieces)

    parts = part.reshape(feat_count, rows // feat_count, -1)
    terms = lax.all_to_all(parts, "feat", 0, 0)
    mine = jnp.sum(terms.astype(jnp.float32), axis=0).astype(jnp.bfloat16)
    latent = lax.all_to_all(jnp.broadcast_to(mine[None], parts.shape), "feat", 0, 0).reshape(rows, -1)
    rank_term = jnp.dot(latent, latent_out, preferred_element_type=jnp.float32).astype(jnp.bfloat16)
    return hidden, rank_term


def solution(mesh):
    placed = (
        P("tok", "feat"),
        P("feat", None, "tok", None),
        P("feat", None, "tok", None),
        P("feat", None),
        P("feat", None),
        P(),
        P("feat", None),
        P(None, "feat"),
    )
    return jax.shard_map(
        per_device,
        mesh=mesh,
        in_specs=placed,
        out_specs=(P("tok", "feat"), P("tok", "feat")),
        check_vma=False,
    )
```

```python
import functools
import jax
import jax.numpy as jnp
from jax import lax
from jax.experimental import pallas as pl
from jax.experimental.pallas import tpu as pltpu
from jax.sharding import PartitionSpec as P

GROUP = 4
SMEM = pl.BlockSpec(memory_space=pltpu.SMEM)
VMEM = pl.BlockSpec(memory_space=pltpu.VMEM)
VMEM_BYTES = 30 * 2**20
SMALL_BYTES = 16 * 2**20


def swapped(value, axis, mask):
    return lax.ppermute(value, axis, [(i, i ^ mask) for i in range(lax.axis_size(axis))])


def shifted(value, step):
    count = lax.axis_size("tok")
    return lax.ppermute(value, "tok", [(i, (i + step * GROUP) % count) for i in range(count)])


def pack_kernel(own_ref, gate_ref, up_ref, *out_refs):
    half = gate_ref.shape[3] // 2
    for m in range(4):
        to = own_ref[0] ^ m
        at = pl.ds(pl.multiple_of(to % 2 * half, 128), half)
        for side, ref in enumerate((gate_ref, up_ref)):
            out_refs[m][side] = ref[to // 2, :, :, at]


def place_kernel(own_ref, *refs):
    for m in range(4):
        refs[4][:, :, own_ref[0] ^ m] = refs[m][...]


def halves_kernel(f_ref, b_ref, f_out, b_out):
    f_out[...] = f_ref[...]
    b_out[...] = b_ref[...]


def block_of_rows(own_refs, partner_refs, j, m, x_lo, start, width):
    blk = partner_refs[0].shape[1]
    rows = own_refs[0].shape[0]
    if j < 2 and m < 2:
        return own_refs[m][:, pl.ds(pl.multiple_of((x_lo ^ j) * blk + start, 128), width)]
    column = pl.ds(pl.multiple_of(start, 128), width)
    if j < 2:
        return own_refs[2 * m - 2 + j][:, column]
    return partner_refs[m % 2 * 3 + j - 2][pl.ds(m // 2 * rows, rows), column]


def last_window(z, z_count, share, blk, window):
    row = (z + z_count // 2) % z_count * share
    return row, jnp.minimum(row // 128 * 128, blk - window)


def early_kernel(place_ref, gs_ref, us_ref, *refs, z_count, window):
    n_w = z_count - 1
    w_refs, own_refs, partner_refs = refs[:n_w], refs[n_w : n_w + 6], refs[n_w + 6 : n_w + 12]
    acc, windows, w_mem = refs[n_w + 12 :]
    x_lo, z = place_ref[5], place_ref[6]
    blk, both = w_mem.shape[1:]
    share, width = blk // z_count, both // 2
    row, start = last_window(z, z_count, share, blk, window)
    last = pl.ds(pl.multiple_of(row, 16), share)
    for j in range(5):
        slot = place_ref[j]
        w_mem[j % 2, last] = jnp.zeros((share, both), w_mem.dtype)
        for i, ref in enumerate(w_refs):
            origin = z - (i + 1) // 2 if i % 2 else z + i // 2
            at = pl.ds(pl.multiple_of((origin + z_count) % z_count * share, 16), share)
            for side in range(2):
                w_mem[j % 2, at, side * width : (side + 1) * width] = ref[side, slot]
        for m in range(4):
            at = pl.ds(m * own_refs[0].shape[0], own_refs[0].shape[0])
            windows[j, at] = block_of_rows(own_refs, partner_refs, j, m, x_lo, start, window)
        x = jnp.concatenate([block_of_rows(own_refs, partner_refs, j, m, x_lo, 0, blk) for m in range(4)])
        term = jnp.dot(x, w_mem[j % 2], preferred_element_type=jnp.float32)
        g, u = term[:, :width] * gs_ref[slot], term[:, width:] * us_ref[slot]
        if j == 0:
            acc[:, :width] = g
            acc[:, width:] = u
        else:
            acc[:, :width] += g
            acc[:, width:] += u


def early(place, gs, us, weights, own_rows, partner_rows):
    blk = own_rows[0].shape[1] // 2
    rows = 4 * own_rows[0].shape[0]
    _, slots, share, width = weights[0].shape
    window = min(2 * 128 * ((share + 127) // 128), blk)
    return pl.pallas_call(
        functools.partial(early_kernel, z_count=blk // share, window=window),
        out_shape=[
            jax.ShapeDtypeStruct((rows, 2 * width), jnp.float32),
            jax.ShapeDtypeStruct((slots, rows, window), jnp.bfloat16),
        ],
        in_specs=[SMEM] * 3 + [VMEM] * (len(weights) + 12),
        out_specs=[VMEM] * 2,
        scratch_shapes=[pltpu.VMEM((2, blk, 2 * width), jnp.bfloat16)],
        compiler_params=pltpu.CompilerParams(vmem_limit_bytes=VMEM_BYTES),
        cost_estimate=pl.CostEstimate(flops=2**33, bytes_accessed=2**20, transcendentals=0),
    )(place, gs, us, *weights, *own_rows, *partner_rows)


def late_kernel(place_ref, gs_ref, us_ref, *refs, z_count, first):
    w_refs, acc_ref, window_ref, out_refs = refs[:2], refs[2], refs[3], refs[4:6]
    w_mem, acc = refs[6:]
    z = place_ref[6]
    share, width = w_refs[0].shape[2:]
    slots, rows, window = window_ref.shape
    rows //= 4
    row, start = last_window(z, z_count, share, z_count * share, window)
    at = pl.ds(pl.multiple_of(row - start, 16), share)
    w_mem[...] = jnp.zeros_like(w_mem)
    mine = [pl.ds((2 * first + core) * rows, rows) for core in range(2)]
    for core in range(2):
        acc[pl.ds(core * rows, rows)] = acc_ref[mine[core]]
    for j in range(slots):
        slot = place_ref[j]
        for side in range(2):
            w_mem[j, at, side * width : (side + 1) * width] = w_refs[side][0, slot]
        x = jnp.concatenate([window_ref[j, at_core] for at_core in mine])
        term = jnp.dot(x, w_mem[j], preferred_element_type=jnp.float32)
        acc[:, :width] += term[:, :width] * gs_ref[slot]
        acc[:, width:] += term[:, width:] * us_ref[slot]
    g = acc[:, :width]
    out = (g / (1.0 + jnp.exp(-g)) * acc[:, width:]).astype(jnp.bfloat16)
    out_refs[0][...] = out[:rows]
    out_refs[1][...] = out[rows:]


def late(place, gs, us, weights, acc, windows, z_count, first):
    slots, rows, window = windows.shape
    rows //= 4
    width = weights[0].shape[3]
    return pl.pallas_call(
        functools.partial(late_kernel, z_count=z_count, first=first),
        out_shape=[jax.ShapeDtypeStruct((rows, width), jnp.bfloat16)] * 2,
        in_specs=[SMEM] * 3 + [VMEM] * 4,
        out_specs=[VMEM] * 2,
        scratch_shapes=[
            pltpu.VMEM((slots, window, 2 * width), jnp.bfloat16),
            pltpu.VMEM((2 * rows, 2 * width), jnp.float32),
        ],
        compiler_params=pltpu.CompilerParams(vmem_limit_bytes=SMALL_BYTES),
        cost_estimate=pl.CostEstimate(
            flops=2 * 2 * 2 * rows * slots * window * width, bytes_accessed=4 * 2**20, transcendentals=2 * rows * width
        ),
    )(place, gs, us, *weights, acc, windows)


def latent_kernel(own_ref, lin_ref, *refs):
    pieces, hidden_ref, part_ref = refs[:4], refs[4], refs[5]
    width = pieces[0].shape[1]
    total = None
    for m in range(4):
        at = pl.ds(pl.multiple_of((own_ref[0] ^ m) * width, width), width)
        piece = pieces[m][...]
        hidden_ref[:, at] = piece
        term = jnp.dot(piece, lin_ref[at], preferred_element_type=jnp.float32)
        total = term if total is None else total + term
    part_ref[...] = total.astype(jnp.bfloat16)


def per_device(tokens, gate_weight, up_weight, gate_scale, up_scale, partners, latent_in, latent_out):
    rows, features = tokens.shape
    blocks, slots, share, blk = gate_weight.shape
    feat_count = lax.axis_size("feat")
    half = blk // 2
    feat, tok = lax.axis_index("feat"), lax.axis_index("tok")
    member, z = tok % GROUP, tok // GROUP
    x_lo, core = member // 2, member % 2
    block_id = feat * blocks + x_lo

    own = member[None].astype(jnp.int32)
    packed = pl.pallas_call(
        pack_kernel,
        out_shape=[jax.ShapeDtypeStruct((2, slots, share, half), jnp.bfloat16)] * 4,
        in_specs=[SMEM, VMEM, VMEM],
        out_specs=[VMEM] * 4,
        compiler_params=pltpu.CompilerParams(vmem_limit_bytes=SMALL_BYTES),
    )(own, gate_weight, up_weight)

    def place(got):
        shape = got[0].shape
        out = pl.pallas_call(
            place_kernel,
            out_shape=jax.ShapeDtypeStruct(shape[:2] + (4,) + shape[2:], jnp.bfloat16),
            in_specs=[SMEM] + [VMEM] * 4,
            out_specs=VMEM,
            compiler_params=pltpu.CompilerParams(vmem_limit_bytes=SMALL_BYTES),
        )(own, *got)
        return out.reshape(shape[:2] + (4 * shape[2],) + shape[3:])

    def block_of(value, which):
        return lax.dynamic_slice(value, (0, which * blk), (rows, blk))

    def step(forward, back):
        return shifted(forward, 1), shifted(back, -1)

    far = [swapped(packed[m], "tok", m) for m in (2, 3)]
    near = swapped(packed[1], "tok", 1)
    w0 = place([packed[0], near, *far])
    barrier = lax.optimization_barrier
    first, other = block_of(tokens, x_lo), block_of(tokens, 1 - x_lo)
    p0_y1, p0_y2 = swapped(first, "feat", 2), swapped(first, "feat", 4)
    w0, other, later = barrier((w0, other, tokens))
    w1 = step(w0, w0)
    s2_own = swapped(other, "tok", 2)
    first, s2_own, p0_y1, p0_y2 = barrier((first, s2_own, p0_y1, p0_y2))
    s2_other = swapped(first, "tok", 2)
    p2_y1 = swapped(s2_own, "feat", 2)
    w1, s2_own, s2_other, p0_y1, p0_y2, p2_y1, first, later = barrier(
        (w1, s2_own, s2_other, p0_y1, p0_y2, p2_y1, first, later)
    )
    w2 = step(*w1)
    p_x = swapped(jnp.concatenate([first, s2_own]), "feat", 1)
    p2_y2 = swapped(s2_own, "feat", 4)
    s1 = swapped(later, "tok", 1)
    s1, s2_other = barrier((s1, s2_other))
    s3_other = swapped(s2_other, "tok", 1)
    p_y1 = jnp.concatenate([p0_y1, p2_y1])
    w2, p_x, p2_y2, p0_y2, p_y1, s2_own, s1, s3_other = barrier((w2, p_x, p2_y2, p0_y2, p_y1, s2_own, s1, s3_other))
    w3 = step(*w2)
    p_y2 = jnp.concatenate([p0_y2, p2_y2])
    q_y1 = swapped(p_y1, "tok", 1)
    q_y1, s2_own = barrier((q_y1, s2_own))
    s3_own = swapped(s2_own, "tok", 1)
    partner_rows = [p_x, p_y1, p_y2, swapped(p_x, "tok", 1), q_y1, swapped(p_y2, "tok", 1)]
    own_rows = [later, s1, s2_own, s2_other, s3_own, s3_other]
    w3, own_rows, partner_rows = barrier((w3, own_rows, partner_rows))
    half_shape = (1,) + w3[0].shape[1:]
    cut = pl.pallas_call(
        halves_kernel,
        grid=(1,),
        out_shape=[jax.ShapeDtypeStruct(half_shape, jnp.bfloat16)] * 2,
        in_specs=[pl.BlockSpec(half_shape, lambda i: (0, 0, 0, 0)), pl.BlockSpec(half_shape, lambda i: (1, 0, 0, 0))],
        out_specs=[pl.BlockSpec(half_shape, lambda i: (0, 0, 0, 0))] * 2,
        compiler_params=pltpu.CompilerParams(vmem_limit_bytes=SMALL_BYTES),
    )(*w3)
    w4 = step(*cut)

    wanted = lax.dynamic_index_in_dim(partners, block_id, 0, keepdims=False)
    labels = block_id ^ jnp.array([0, 1, 2, 4, 8], jnp.int32)
    order = jnp.sum(jnp.where(labels[:, None] == wanted[None, :], jnp.arange(5, dtype=jnp.int32)[None, :], 0), axis=1)
    here = jnp.concatenate([order, jnp.stack([x_lo, z]).astype(jnp.int32)])
    gs = lax.dynamic_index_in_dim(gate_scale, x_lo, 0, keepdims=False)
    us = lax.dynamic_index_in_dim(up_scale, x_lo, 0, keepdims=False)

    acc, windows = early(here, gs, us, (w0, *w1, *w2, *w3), own_rows, partner_rows)
    z_count = lax.axis_size("tok") // GROUP
    made = late(here, gs, us, w4, acc, windows, z_count, 1)
    far_hidden = [swapped(v, "tok", mask) for v, mask in zip(made, (2, 3))]
    made = late(here, gs, us, w4, acc, windows, z_count, 0)
    hidden_pieces = [made[0], swapped(made[1], "tok", 1), *far_hidden]
    hidden, part = pl.pallas_call(
        latent_kernel,
        out_shape=(
            jax.ShapeDtypeStruct((rows, features), jnp.bfloat16),
            jax.ShapeDtypeStruct((rows, latent_in.shape[1]), jnp.bfloat16),
        ),
        in_specs=[SMEM] + [VMEM] * 5,
        out_specs=(VMEM, VMEM),
        compiler_params=pltpu.CompilerParams(vmem_limit_bytes=SMALL_BYTES),
        cost_estimate=pl.CostEstimate(flops=2 * rows * features * latent_in.shape[1], bytes_accessed=4 * 2**20, transcendentals=0),
    )(own, latent_in, *hidden_pieces)

    parts = part.reshape(feat_count, rows // feat_count, -1)
    terms = lax.all_to_all(parts, "feat", 0, 0)
    mine = jnp.sum(terms.astype(jnp.float32), axis=0).astype(jnp.bfloat16)
    latent = lax.all_to_all(jnp.broadcast_to(mine[None], parts.shape), "feat", 0, 0).reshape(rows, -1)
    rank_term = jnp.dot(latent, latent_out, preferred_element_type=jnp.float32).astype(jnp.bfloat16)
    return hidden, rank_term


def solution(mesh):
    placed = (
        P("tok", "feat"),
        P("feat", None, "tok", None),
        P("feat", None, "tok", None),
        P("feat", None),
        P("feat", None),
        P(),
        P("feat", None),
        P(None, "feat"),
    )
    return jax.shard_map(
        per_device,
        mesh=mesh,
        in_specs=placed,
        out_specs=(P("tok", "feat"), P("tok", "feat")),
        check_vma=False,
    )
```

```python
import functools
import jax
import jax.numpy as jnp
from jax import lax
from jax.experimental import pallas as pl
from jax.experimental.pallas import tpu as pltpu
from jax.sharding import PartitionSpec as P

GROUP = 4
SMEM = pl.BlockSpec(memory_space=pltpu.SMEM)
VMEM = pl.BlockSpec(memory_space=pltpu.VMEM)
VMEM_BYTES = 60 * 2**20
SMALL_BYTES = 16 * 2**20


def swapped(value, axis, mask):
    return lax.ppermute(value, axis, [(i, i ^ mask) for i in range(lax.axis_size(axis))])


def shifted(value, step):
    count = lax.axis_size("tok")
    return lax.ppermute(value, "tok", [(i, (i + step * GROUP) % count) for i in range(count)])


def pack_kernel(own_ref, gate_ref, up_ref, *out_refs):
    half = gate_ref.shape[3] // 2
    for m in range(4):
        to = own_ref[0] ^ m
        at = pl.ds(pl.multiple_of(to % 2 * half, 128), half)
        for side, ref in enumerate((gate_ref, up_ref)):
            out_refs[m][side] = ref[to // 2, :, :, at]


def place_kernel(own_ref, *refs):
    for m in range(4):
        refs[4][:, :, own_ref[0] ^ m] = refs[m][...]


def halves_kernel(f_ref, b_ref, f_out, b_out):
    f_out[...] = f_ref[...]
    b_out[...] = b_ref[...]


def block_of_rows(own_refs, partner_refs, j, m, x_lo, start, width):
    blk = partner_refs[0].shape[1]
    rows = own_refs[0].shape[0]
    if j < 2 and m < 2:
        return own_refs[m][:, pl.ds(pl.multiple_of((x_lo ^ j) * blk + start, 128), width)]
    column = pl.ds(pl.multiple_of(start, 128), width)
    if j < 2:
        return own_refs[2 * m - 2 + j][:, column]
    return partner_refs[m % 2 * 3 + j - 2][pl.ds(m // 2 * rows, rows), column]


def last_window(z, z_count, share, blk, window):
    row = (z + z_count // 2) % z_count * share
    return row, jnp.minimum(row // 128 * 128, blk - window)


def lay_kernel(place_ref, *refs, z_count, share):
    own_refs, partner_refs, x_ref, windows = refs[:6], refs[6:12], refs[12], refs[13]
    x_lo, z = place_ref[5], place_ref[6]
    rows, (blk, window) = own_refs[0].shape[0], (x_ref.shape[2], windows.shape[2])
    _, start = last_window(z, z_count, share, blk, window)
    for j in range(5):
        for m in range(4):
            at = pl.ds(m * rows, rows)
            x_ref[j, at] = block_of_rows(own_refs, partner_refs, j, m, x_lo, 0, blk)
            windows[j, at] = block_of_rows(own_refs, partner_refs, j, m, x_lo, start, window)


def lay(place, own_rows, partner_rows, share):
    rows, features = own_rows[0].shape
    blk = features // 2
    window = min(2 * 128 * ((share + 127) // 128), blk)
    return pl.pallas_call(
        functools.partial(lay_kernel, z_count=blk // share, share=share),
        out_shape=[jax.ShapeDtypeStruct((5, 4 * rows, w), jnp.bfloat16) for w in (blk, window)],
        in_specs=[SMEM] + [VMEM] * 12,
        out_specs=[VMEM] * 2,
        compiler_params=pltpu.CompilerParams(vmem_limit_bytes=VMEM_BYTES),
        cost_estimate=pl.CostEstimate(flops=2**20, bytes_accessed=2**20, transcendentals=0),
    )(place, *own_rows, *partner_rows)


def early_kernel(place_ref, gs_ref, us_ref, x_ref, *refs, z_count):
    w_refs, acc, w_mem = refs[: z_count - 1], refs[z_count - 1], refs[z_count]
    j = pl.program_id(0)
    z, slot = place_ref[6], place_ref[j]
    blk, both = w_mem.shape
    share, width = blk // z_count, both // 2
    w_mem[pl.ds(pl.multiple_of((z + z_count // 2) % z_count * share, 16), share)] = jnp.zeros((share, both), w_mem.dtype)
    for i, ref in enumerate(w_refs):
        origin = z - (i + 1) // 2 if i % 2 else z + i // 2
        at = pl.ds(pl.multiple_of((origin + z_count) % z_count * share, 16), share)
        for side in range(2):
            w_mem[at, side * width : (side + 1) * width] = ref[side, 0]
    term = jnp.dot(x_ref[0], w_mem[...], preferred_element_type=jnp.float32)
    g, u = term[:, :width] * gs_ref[slot], term[:, width:] * us_ref[slot]

    @pl.when(j == 0)
    def _():
        acc[:, :width] = g
        acc[:, width:] = u

    @pl.when(j > 0)
    def _():
        acc[:, :width] += g
        acc[:, width:] += u


def early(place, gs, us, weights, x):
    slots, rows, blk = x.shape
    share, width = weights[0].shape[2:]
    return pl.pallas_call(
        functools.partial(early_kernel, z_count=blk // share),
        out_shape=jax.ShapeDtypeStruct((rows, 2 * width), jnp.float32),
        grid_spec=pltpu.PrefetchScalarGridSpec(
            num_scalar_prefetch=3,
            grid=(slots,),
            in_specs=[pl.BlockSpec((1, rows, blk), lambda j, place, *_: (j, 0, 0))]
            + [pl.BlockSpec((2, 1, share, width), lambda j, place, *_: (0, place[j], 0, 0))] * len(weights),
            out_specs=pl.BlockSpec((rows, 2 * width), lambda j, *_: (0, 0)),
            scratch_shapes=[pltpu.VMEM((blk, 2 * width), jnp.bfloat16)],
        ),
        compiler_params=pltpu.CompilerParams(vmem_limit_bytes=VMEM_BYTES),
        cost_estimate=pl.CostEstimate(flops=2**20, bytes_accessed=2**20, transcendentals=0),
    )(place, gs, us, x, *weights)


def late_kernel(place_ref, gs_ref, us_ref, g_ref, u_ref, acc_ref, window_ref, near_ref, far_ref, w_mem, acc, *, z_count):
    z = place_ref[6]
    share, width = g_ref.shape[2:]
    slots, rows, window = window_ref.shape
    rows //= 2
    row, start = last_window(z, z_count, share, z_count * share, window)
    at = pl.ds(pl.multiple_of(row - start, 16), share)
    w_mem[...] = jnp.zeros_like(w_mem)
    for j in range(slots):
        slot = place_ref[j]
        w_mem[j, at, :width] = g_ref[0, slot]
        w_mem[j, at, width:] = u_ref[0, slot]
        term = jnp.dot(window_ref[j], w_mem[j], preferred_element_type=jnp.float32)
        before = acc_ref if j == 0 else acc
        acc[:, :width] = before[:, :width] + term[:, :width] * gs_ref[slot]
        acc[:, width:] = before[:, width:] + term[:, width:] * us_ref[slot]
    g = acc[:, :width]
    out = (g / (1.0 + jnp.exp(-g)) * acc[:, width:]).astype(jnp.bfloat16)
    near_ref[...] = out[:rows]
    far_ref[...] = out[rows:]


def late(place, gs, us, weights, acc, windows, z_count, first):
    slots, rows, window = windows.shape
    rows //= 4
    share, width = weights[0].shape[2:]
    return pl.pallas_call(
        functools.partial(late_kernel, z_count=z_count),
        out_shape=[jax.ShapeDtypeStruct((rows, width), jnp.bfloat16)] * 2,
        grid=(1,),
        in_specs=[SMEM] * 3
        + [pl.BlockSpec((1, slots, share, width), lambda i: (0, 0, 0, 0))] * 2
        + [
            pl.BlockSpec((2 * rows, 2 * width), lambda i: (first, 0)),
            pl.BlockSpec((slots, 2 * rows, window), lambda i: (0, first, 0)),
        ],
        out_specs=[pl.BlockSpec((rows, width), lambda i: (0, 0))] * 2,
        scratch_shapes=[
            pltpu.VMEM((slots, window, 2 * width), jnp.bfloat16),
            pltpu.VMEM((2 * rows, 2 * width), jnp.float32),
        ],
        compiler_params=pltpu.CompilerParams(vmem_limit_bytes=VMEM_BYTES),
        cost_estimate=pl.CostEstimate(
            flops=2 * 2 * 2 * rows * slots * window * width, bytes_accessed=4 * 2**20, transcendentals=2 * rows * width
        ),
    )(place, gs, us, *weights, acc, windows)


def latent_kernel(own_ref, lin_ref, *refs):
    pieces, hidden_ref, part_ref = refs[:4], refs[4], refs[5]
    width = pieces[0].shape[1]
    total = None
    for m in range(4):
        at = pl.ds(pl.multiple_of((own_ref[0] ^ m) * width, width), width)
        piece = pieces[m][...]
        hidden_ref[:, at] = piece
        term = jnp.dot(piece, lin_ref[at], preferred_element_type=jnp.float32)
        total = term if total is None else total + term
    part_ref[...] = total.astype(jnp.bfloat16)


def per_device(tokens, gate_weight, up_weight, gate_scale, up_scale, partners, latent_in, latent_out):
    rows, features = tokens.shape
    blocks, slots, share, blk = gate_weight.shape
    feat_count = lax.axis_size("feat")
    half = blk // 2
    feat, tok = lax.axis_index("feat"), lax.axis_index("tok")
    member, z = tok % GROUP, tok // GROUP
    x_lo, core = member // 2, member % 2
    block_id = feat * blocks + x_lo

    wanted = lax.dynamic_index_in_dim(partners, block_id, 0, keepdims=False)
    labels = block_id ^ jnp.array([0, 1, 2, 4, 8], jnp.int32)
    order = jnp.sum(jnp.where(labels[:, None] == wanted[None, :], jnp.arange(5, dtype=jnp.int32)[None, :], 0), axis=1)
    here = jnp.concatenate([order, jnp.stack([x_lo, z]).astype(jnp.int32)])
    gs = lax.dynamic_index_in_dim(gate_scale, x_lo, 0, keepdims=False)
    us = lax.dynamic_index_in_dim(up_scale, x_lo, 0, keepdims=False)

    own = member[None].astype(jnp.int32)
    packed = pl.pallas_call(
        pack_kernel,
        out_shape=[jax.ShapeDtypeStruct((2, slots, share, half), jnp.bfloat16)] * 4,
        in_specs=[SMEM, VMEM, VMEM],
        out_specs=[VMEM] * 4,
        compiler_params=pltpu.CompilerParams(vmem_limit_bytes=SMALL_BYTES),
    )(own, gate_weight, up_weight)

    def place(got):
        shape = got[0].shape
        out = pl.pallas_call(
            place_kernel,
            out_shape=jax.ShapeDtypeStruct(shape[:2] + (4,) + shape[2:], jnp.bfloat16),
            in_specs=[SMEM] + [VMEM] * 4,
            out_specs=VMEM,
            compiler_params=pltpu.CompilerParams(vmem_limit_bytes=SMALL_BYTES),
        )(own, *got)
        return out.reshape(shape[:2] + (4 * shape[2],) + shape[3:])

    def block_of(value, which):
        return lax.dynamic_slice(value, (0, which * blk), (rows, blk))

    def step(forward, back):
        return shifted(forward, 1), shifted(back, -1)

    far = [swapped(packed[m], "tok", m) for m in (2, 3)]
    near = swapped(packed[1], "tok", 1)
    w0 = place([packed[0], near, *far])
    barrier = lax.optimization_barrier
    first, other = block_of(tokens, x_lo), block_of(tokens, 1 - x_lo)
    p0_y1, p0_y2 = swapped(first, "feat", 2), swapped(first, "feat", 4)
    w0, other, later = barrier((w0, other, tokens))
    w1 = step(w0, w0)
    s2_own = swapped(other, "tok", 2)
    first, s2_own, p0_y1, p0_y2 = barrier((first, s2_own, p0_y1, p0_y2))
    s2_other = swapped(first, "tok", 2)
    p2_y1 = swapped(s2_own, "feat", 2)
    w1, s2_own, s2_other, p0_y1, p0_y2, p2_y1, first, later = barrier(
        (w1, s2_own, s2_other, p0_y1, p0_y2, p2_y1, first, later)
    )
    w2 = step(*w1)
    p_x = swapped(jnp.concatenate([first, s2_own]), "feat", 1)
    p2_y2 = swapped(s2_own, "feat", 4)
    s1 = swapped(later, "tok", 1)
    s1, s2_other = barrier((s1, s2_other))
    s3_other = swapped(s2_other, "tok", 1)
    p_y1 = jnp.concatenate([p0_y1, p2_y1])
    w2, p_x, p2_y2, p0_y2, p_y1, s2_own, s1, s3_other = barrier((w2, p_x, p2_y2, p0_y2, p_y1, s2_own, s1, s3_other))
    w3 = step(*w2)
    p_y2 = jnp.concatenate([p0_y2, p2_y2])
    q_y1 = swapped(p_y1, "tok", 1)
    q_y1, s2_own = barrier((q_y1, s2_own))
    s3_own = swapped(s2_own, "tok", 1)
    partner_rows = [p_x, p_y1, p_y2, swapped(p_x, "tok", 1), q_y1, swapped(p_y2, "tok", 1)]
    own_rows = [later, s1, s2_own, s2_other, s3_own, s3_other]
    x, windows = lay(here, own_rows, partner_rows, w0.shape[2])
    w3, x, windows = barrier((w3, x, windows))
    half_shape = (1,) + w3[0].shape[1:]
    cut = pl.pallas_call(
        halves_kernel,
        grid=(1,),
        out_shape=[jax.ShapeDtypeStruct(half_shape, jnp.bfloat16)] * 2,
        in_specs=[pl.BlockSpec(half_shape, lambda i: (0, 0, 0, 0)), pl.BlockSpec(half_shape, lambda i: (1, 0, 0, 0))],
        out_specs=[pl.BlockSpec(half_shape, lambda i: (0, 0, 0, 0))] * 2,
        compiler_params=pltpu.CompilerParams(vmem_limit_bytes=SMALL_BYTES),
    )(*w3)
    w4 = step(*cut)

    acc = early(here, gs, us, (w0, *w1, *w2, *w3), x)
    z_count = lax.axis_size("tok") // GROUP
    made = late(here, gs, us, w4, acc, windows, z_count, 1)
    far_hidden = [swapped(v, "tok", mask) for v, mask in zip(made, (2, 3))]
    made = late(here, gs, us, w4, acc, windows, z_count, 0)
    hidden_pieces = [made[0], swapped(made[1], "tok", 1), *far_hidden]
    hidden, part = pl.pallas_call(
        latent_kernel,
        out_shape=(
            jax.ShapeDtypeStruct((rows, features), jnp.bfloat16),
            jax.ShapeDtypeStruct((rows, latent_in.shape[1]), jnp.bfloat16),
        ),
        in_specs=[SMEM] + [VMEM] * 5,
        out_specs=(VMEM, VMEM),
        compiler_params=pltpu.CompilerParams(vmem_limit_bytes=SMALL_BYTES),
        cost_estimate=pl.CostEstimate(flops=2 * rows * features * latent_in.shape[1], bytes_accessed=4 * 2**20, transcendentals=0),
    )(own, latent_in, *hidden_pieces)

    parts = part.reshape(feat_count, rows // feat_count, -1)
    terms = lax.all_to_all(parts, "feat", 0, 0)
    mine = jnp.sum(terms.astype(jnp.float32), axis=0).astype(jnp.bfloat16)
    latent = lax.all_to_all(jnp.broadcast_to(mine[None], parts.shape), "feat", 0, 0).reshape(rows, -1)
    rank_term = jnp.dot(latent, latent_out, preferred_element_type=jnp.float32).astype(jnp.bfloat16)
    return hidden, rank_term


def solution(mesh):
    placed = (
        P("tok", "feat"),
        P("feat", None, "tok", None),
        P("feat", None, "tok", None),
        P("feat", None),
        P("feat", None),
        P(),
        P("feat", None),
        P(None, "feat"),
    )
    return jax.shard_map(
        per_device,
        mesh=mesh,
        in_specs=placed,
        out_specs=(P("tok", "feat"), P("tok", "feat")),
        check_vma=False,
    )
```

```python
import functools
import jax
import jax.numpy as jnp
from jax import lax
from jax.experimental import pallas as pl
from jax.experimental.pallas import tpu as pltpu
from jax.sharding import PartitionSpec as P

GROUP = 4
ANY = pl.BlockSpec(memory_space=pl.ANY)
SMEM = pl.BlockSpec(memory_space=pltpu.SMEM)
VMEM = pl.BlockSpec(memory_space=pltpu.VMEM)
VMEM_BYTES = 44 * 2**20
LAY_BYTES = 60 * 2**20
SMALL_BYTES = 16 * 2**20


def swapped(value, axis, mask):
    return lax.ppermute(value, axis, [(i, i ^ mask) for i in range(lax.axis_size(axis))])


def shifted(value, step):
    count = lax.axis_size("tok")
    return lax.ppermute(value, "tok", [(i, (i + step * GROUP) % count) for i in range(count)])


def pack_kernel(own_ref, gate_ref, up_ref, *out_refs):
    half = gate_ref.shape[3] // 2
    for m in range(4):
        to = own_ref[0] ^ m
        at = pl.ds(pl.multiple_of(to % 2 * half, 128), half)
        for side, ref in enumerate((gate_ref, up_ref)):
            out_refs[m][side] = ref[to // 2, :, :, at]


def place_kernel(own_ref, *refs):
    for m in range(4):
        refs[4][:, :, own_ref[0] ^ m] = refs[m][...]


def halves_kernel(f_ref, b_ref, f_out, b_out):
    f_out[...] = f_ref[...]
    b_out[...] = b_ref[...]


def block_of_rows(own_refs, partner_refs, j, m, x_lo, start, width):
    blk = partner_refs[0].shape[1]
    rows = own_refs[0].shape[0]
    if j < 2 and m < 2:
        return own_refs[m][:, pl.ds(pl.multiple_of((x_lo ^ j) * blk + start, 128), width)]
    column = pl.ds(pl.multiple_of(start, 128), width)
    if j < 2:
        return own_refs[2 * m - 2 + j][:, column]
    return partner_refs[m % 2 * 3 + j - 2][pl.ds(m // 2 * rows, rows), column]


def last_window(z, z_count, share, blk, window):
    row = (z + z_count // 2) % z_count * share
    return row, jnp.minimum(row // 128 * 128, blk - window)


def ring_row(i, z, z_count, share):
    origin = z - (i + 1) // 2 if i % 2 else z + i // 2
    return pl.ds(pl.multiple_of((origin + z_count) % z_count * share, 16), share)


def lay_kernel(place_ref, *refs, z_count, n_w):
    w_refs, own_refs, partner_refs = refs[:n_w], refs[n_w : n_w + 6], refs[n_w + 6 : n_w + 12]
    x_ref, windows, w_out = refs[n_w + 12 :]
    x_lo, z = place_ref[5], place_ref[6]
    share, width = w_refs[0].shape[2:]
    rows, (blk, window) = own_refs[0].shape[0], (x_ref.shape[2], windows.shape[2])
    _, start = last_window(z, z_count, share, blk, window)
    for j in range(5):
        for m in range(4):
            at = pl.ds(m * rows, rows)
            x_ref[j, at] = block_of_rows(own_refs, partner_refs, j, m, x_lo, 0, blk)
            windows[j, at] = block_of_rows(own_refs, partner_refs, j, m, x_lo, start, window)
        for i in range(z_count):
            at = ring_row(i, z, z_count, share)
            for side in range(2):
                piece = w_refs[i][side, place_ref[j]] if i < n_w else jnp.zeros((share, width), w_out.dtype)
                w_out[j, at, side * width : (side + 1) * width] = piece


def lay(place, weights, own_rows, partner_rows):
    rows, features = own_rows[0].shape
    blk = features // 2
    share, width = weights[0].shape[2:]
    window = min(2 * 128 * ((share + 127) // 128), blk)
    shapes = [(5, 4 * rows, blk), (5, 4 * rows, window), (5, blk, 2 * width)]
    return pl.pallas_call(
        functools.partial(lay_kernel, z_count=blk // share, n_w=len(weights)),
        out_shape=[jax.ShapeDtypeStruct(shape, jnp.bfloat16) for shape in shapes],
        in_specs=[SMEM] + [VMEM] * (len(weights) + 12),
        out_specs=[VMEM] * 3,
        compiler_params=pltpu.CompilerParams(vmem_limit_bytes=LAY_BYTES),
        cost_estimate=pl.CostEstimate(flops=2**20, bytes_accessed=2**20, transcendentals=0),
    )(place, *weights, *own_rows, *partner_rows)


def early_kernel(place_ref, gs_ref, us_ref, x_ref, w_ref, below_ref, above_ref, acc, x_mem, w_mem, x_sem, w_sem, *, z_count):
    z = place_ref[6]
    blk, both = w_mem.shape[1:]
    share, width = blk // z_count, both // 2
    copies = []
    for j in range(5):
        copies.append(pltpu.make_async_copy(w_ref.at[j], w_mem.at[j], w_sem.at[j]))
        copies.append(pltpu.make_async_copy(x_ref.at[j], x_mem.at[j], x_sem.at[j]))
    for copy in copies:
        copy.start()
    for j in range(5):
        slot = place_ref[j]
        copies[2 * j].wait()
        for i, ref in ((z_count - 3, below_ref), (z_count - 2, above_ref)):
            at = ring_row(i, z, z_count, share)
            for side in range(2):
                w_mem[j, at, side * width : (side + 1) * width] = ref[side, slot]
        copies[2 * j + 1].wait()
        term = jnp.dot(x_mem[j], w_mem[j], preferred_element_type=jnp.float32)
        g, u = term[:, :width] * gs_ref[slot], term[:, width:] * us_ref[slot]
        if j == 0:
            acc[:, :width] = g
            acc[:, width:] = u
        else:
            acc[:, :width] += g
            acc[:, width:] += u


def early(place, gs, us, x, weights, below, above):
    slots, rows, blk = x.shape
    share, width = below.shape[2:]
    return pl.pallas_call(
        functools.partial(early_kernel, z_count=blk // share),
        out_shape=jax.ShapeDtypeStruct((rows, 2 * width), jnp.float32),
        in_specs=[SMEM] * 3 + [ANY] * 2 + [VMEM] * 2,
        out_specs=VMEM,
        scratch_shapes=[
            pltpu.VMEM(x.shape, jnp.bfloat16),
            pltpu.VMEM(weights.shape, jnp.bfloat16),
            pltpu.SemaphoreType.DMA((slots,)),
            pltpu.SemaphoreType.DMA((slots,)),
        ],
        compiler_params=pltpu.CompilerParams(vmem_limit_bytes=VMEM_BYTES),
        cost_estimate=pl.CostEstimate(flops=2**20, bytes_accessed=2**20, transcendentals=0),
    )(place, gs, us, x, weights, below, above)


def late_kernel(place_ref, gs_ref, us_ref, g_ref, u_ref, acc_ref, window_ref, near_ref, far_ref, w_mem, acc, *, z_count):
    z = place_ref[6]
    share, width = g_ref.shape[2:]
    slots, rows, window = window_ref.shape
    rows //= 2
    row, start = last_window(z, z_count, share, z_count * share, window)
    at = pl.ds(pl.multiple_of(row - start, 16), share)
    w_mem[...] = jnp.zeros_like(w_mem)
    for j in range(slots):
        slot = place_ref[j]
        w_mem[j, at, :width] = g_ref[0, slot]
        w_mem[j, at, width:] = u_ref[0, slot]
        term = jnp.dot(window_ref[j], w_mem[j], preferred_element_type=jnp.float32)
        before = acc_ref if j == 0 else acc
        acc[:, :width] = before[:, :width] + term[:, :width] * gs_ref[slot]
        acc[:, width:] = before[:, width:] + term[:, width:] * us_ref[slot]
    g = acc[:, :width]
    out = (g / (1.0 + jnp.exp(-g)) * acc[:, width:]).astype(jnp.bfloat16)
    near_ref[...] = out[:rows]
    far_ref[...] = out[rows:]


def late(place, gs, us, weights, acc, windows, z_count, first):
    slots, rows, window = windows.shape
    rows //= 4
    share, width = weights[0].shape[2:]
    return pl.pallas_call(
        functools.partial(late_kernel, z_count=z_count),
        out_shape=[jax.ShapeDtypeStruct((rows, width), jnp.bfloat16)] * 2,
        grid=(1,),
        in_specs=[SMEM] * 3
        + [pl.BlockSpec((1, slots, share, width), lambda i: (0, 0, 0, 0))] * 2
        + [
            pl.BlockSpec((2 * rows, 2 * width), lambda i: (first, 0)),
            pl.BlockSpec((slots, 2 * rows, window), lambda i: (0, first, 0)),
        ],
        out_specs=[pl.BlockSpec((rows, width), lambda i: (0, 0))] * 2,
        scratch_shapes=[
            pltpu.VMEM((slots, window, 2 * width), jnp.bfloat16),
            pltpu.VMEM((2 * rows, 2 * width), jnp.float32),
        ],
        compiler_params=pltpu.CompilerParams(vmem_limit_bytes=VMEM_BYTES),
        cost_estimate=pl.CostEstimate(
            flops=2 * 2 * 2 * rows * slots * window * width, bytes_accessed=4 * 2**20, transcendentals=2 * rows * width
        ),
    )(place, gs, us, *weights, acc, windows)


def latent_kernel(own_ref, lin_ref, *refs):
    pieces, hidden_ref, part_ref, total = refs[:4], refs[4], refs[5], refs[6]
    step = pl.program_id(0)
    for m in range(4):

        @pl.when(step == m)
        def _(m=m):
            piece = pieces[m][...]
            hidden_ref[...] = piece
            term = jnp.dot(piece, lin_ref[...], preferred_element_type=jnp.float32)
            if m > 0:
                term += total[...]
            if m < 3:
                total[...] = term
            else:
                part_ref[...] = term.astype(jnp.bfloat16)


def per_device(tokens, gate_weight, up_weight, gate_scale, up_scale, partners, latent_in, latent_out):
    rows, features = tokens.shape
    blocks, slots, share, blk = gate_weight.shape
    feat_count = lax.axis_size("feat")
    half = blk // 2
    feat, tok = lax.axis_index("feat"), lax.axis_index("tok")
    member, z = tok % GROUP, tok // GROUP
    x_lo, core = member // 2, member % 2
    block_id = feat * blocks + x_lo

    wanted = lax.dynamic_index_in_dim(partners, block_id, 0, keepdims=False)
    labels = block_id ^ jnp.array([0, 1, 2, 4, 8], jnp.int32)
    order = jnp.sum(jnp.where(labels[:, None] == wanted[None, :], jnp.arange(5, dtype=jnp.int32)[None, :], 0), axis=1)
    here = jnp.concatenate([order, jnp.stack([x_lo, z]).astype(jnp.int32)])
    gs = lax.dynamic_index_in_dim(gate_scale, x_lo, 0, keepdims=False)
    us = lax.dynamic_index_in_dim(up_scale, x_lo, 0, keepdims=False)

    own = member[None].astype(jnp.int32)
    packed = pl.pallas_call(
        pack_kernel,
        out_shape=[jax.ShapeDtypeStruct((2, slots, share, half), jnp.bfloat16)] * 4,
        in_specs=[SMEM, VMEM, VMEM],
        out_specs=[VMEM] * 4,
        compiler_params=pltpu.CompilerParams(vmem_limit_bytes=LAY_BYTES),
    )(own, gate_weight, up_weight)

    def place(got):
        shape = got[0].shape
        out = pl.pallas_call(
            place_kernel,
            out_shape=jax.ShapeDtypeStruct(shape[:2] + (4,) + shape[2:], jnp.bfloat16),
            in_specs=[SMEM] + [VMEM] * 4,
            out_specs=VMEM,
            compiler_params=pltpu.CompilerParams(vmem_limit_bytes=LAY_BYTES),
        )(own, *got)
        return out.reshape(shape[:2] + (4 * shape[2],) + shape[3:])

    def block_of(value, which):
        return lax.dynamic_slice(value, (0, which * blk), (rows, blk))

    def step(forward, back):
        return shifted(forward, 1), shifted(back, -1)

    far = [swapped(packed[m], "tok", m) for m in (2, 3)]
    near = swapped(packed[1], "tok", 1)
    w0 = place([packed[0], near, *far])
    barrier = lax.optimization_barrier
    first, other = block_of(tokens, x_lo), block_of(tokens, 1 - x_lo)
    p0_y1, p0_y2 = swapped(first, "feat", 2), swapped(first, "feat", 4)
    w0, other, later = barrier((w0, other, tokens))
    w1 = step(w0, w0)
    s2_own = swapped(other, "tok", 2)
    first, s2_own, p0_y1, p0_y2 = barrier((first, s2_own, p0_y1, p0_y2))
    s2_other = swapped(first, "tok", 2)
    p2_y1 = swapped(s2_own, "feat", 2)
    w1, s2_own, s2_other, p0_y1, p0_y2, p2_y1, first, later = barrier(
        (w1, s2_own, s2_other, p0_y1, p0_y2, p2_y1, first, later)
    )
    w2 = step(*w1)
    p_x = swapped(jnp.concatenate([first, s2_own]), "feat", 1)
    p2_y2 = swapped(s2_own, "feat", 4)
    s1 = swapped(later, "tok", 1)
    s1, s2_other = barrier((s1, s2_other))
    s3_other = swapped(s2_other, "tok", 1)
    p_y1 = jnp.concatenate([p0_y1, p2_y1])
    w2, p_x, p2_y2, p0_y2, p_y1, s2_own, s1, s3_other = barrier((w2, p_x, p2_y2, p0_y2, p_y1, s2_own, s1, s3_other))
    w3 = step(*w2)
    p_y2 = jnp.concatenate([p0_y2, p2_y2])
    q_y1 = swapped(p_y1, "tok", 1)
    q_y1, s2_own = barrier((q_y1, s2_own))
    s3_own = swapped(s2_own, "tok", 1)
    partner_rows = [p_x, p_y1, p_y2, swapped(p_x, "tok", 1), q_y1, swapped(p_y2, "tok", 1)]
    own_rows = [later, s1, s2_own, s2_other, s3_own, s3_other]
    x, windows, w_laid = lay(here, (w0, *w1, *w2), own_rows, partner_rows)
    w3, x, windows, w_laid = barrier((w3, x, windows, w_laid))
    half_shape = (1,) + w3[0].shape[1:]
    cut = pl.pallas_call(
        halves_kernel,
        grid=(1,),
        out_shape=[jax.ShapeDtypeStruct(half_shape, jnp.bfloat16)] * 2,
        in_specs=[pl.BlockSpec(half_shape, lambda i: (0, 0, 0, 0)), pl.BlockSpec(half_shape, lambda i: (1, 0, 0, 0))],
        out_specs=[pl.BlockSpec(half_shape, lambda i: (0, 0, 0, 0))] * 2,
        compiler_params=pltpu.CompilerParams(vmem_limit_bytes=SMALL_BYTES),
    )(*w3)
    w4 = step(*cut)

    acc = early(here, gs, us, x, w_laid, *w3)
    z_count = lax.axis_size("tok") // GROUP
    made = late(here, gs, us, w4, acc, windows, z_count, 1)
    far_hidden = [swapped(v, "tok", mask) for v, mask in zip(made, (2, 3))]
    made = late(here, gs, us, w4, acc, windows, z_count, 0)
    hidden_pieces = [made[0], swapped(made[1], "tok", 1), *far_hidden]
    rank = latent_in.shape[1]
    hidden, part = pl.pallas_call(
        latent_kernel,
        out_shape=(
            jax.ShapeDtypeStruct((rows, features), jnp.bfloat16),
            jax.ShapeDtypeStruct((rows, rank), jnp.bfloat16),
        ),
        grid_spec=pltpu.PrefetchScalarGridSpec(
            num_scalar_prefetch=1,
            grid=(4,),
            in_specs=[pl.BlockSpec((half, rank), lambda m, own: (own[0] ^ m, 0))]
            + [pl.BlockSpec((rows, half), lambda m, own: (0, 0))] * 4,
            out_specs=[
                pl.BlockSpec((rows, half), lambda m, own: (0, own[0] ^ m)),
                pl.BlockSpec((rows, rank), lambda m, own: (0, 0)),
            ],
            scratch_shapes=[pltpu.VMEM((rows, rank), jnp.float32)],
        ),
        compiler_params=pltpu.CompilerParams(vmem_limit_bytes=VMEM_BYTES),
        cost_estimate=pl.CostEstimate(flops=2 * rows * features * rank, bytes_accessed=4 * 2**20, transcendentals=0),
    )(own, latent_in, *hidden_pieces)

    parts = part.reshape(feat_count, rows // feat_count, -1)
    terms = lax.all_to_all(parts, "feat", 0, 0)
    mine = jnp.sum(terms.astype(jnp.float32), axis=0).astype(jnp.bfloat16)
    latent = lax.all_to_all(jnp.broadcast_to(mine[None], parts.shape), "feat", 0, 0).reshape(rows, -1)
    rank_term = jnp.dot(latent, latent_out, preferred_element_type=jnp.float32).astype(jnp.bfloat16)
    return hidden, rank_term


def solution(mesh):
    placed = (
        P("tok", "feat"),
        P("feat", None, "tok", None),
        P("feat", None, "tok", None),
        P("feat", None),
        P("feat", None),
        P(),
        P("feat", None),
        P(None, "feat"),
    )
    return jax.shard_map(
        per_device,
        mesh=mesh,
        in_specs=placed,
        out_specs=(P("tok", "feat"), P("tok", "feat")),
        check_vma=False,
    )
```

```python
import functools
import jax
import jax.numpy as jnp
from jax import lax
from jax.experimental import pallas as pl
from jax.experimental.pallas import tpu as pltpu
from jax.sharding import PartitionSpec as P

GROUP = 4
ANY = pl.BlockSpec(memory_space=pl.ANY)
SMEM = pl.BlockSpec(memory_space=pltpu.SMEM)
VMEM = pl.BlockSpec(memory_space=pltpu.VMEM)
VMEM_BYTES = 44 * 2**20
LAY_BYTES = 60 * 2**20
SMALL_BYTES = 16 * 2**20


def swapped(value, axis, mask):
    return lax.ppermute(value, axis, [(i, i ^ mask) for i in range(lax.axis_size(axis))])


def shifted(value, step):
    count = lax.axis_size("tok")
    return lax.ppermute(value, "tok", [(i, (i + step * GROUP) % count) for i in range(count)])


def pack_kernel(own_ref, gate_ref, up_ref, *out_refs):
    half = gate_ref.shape[3] // 2
    for m in range(4):
        to = own_ref[0] ^ m
        at = pl.ds(pl.multiple_of(to % 2 * half, 128), half)
        for side, ref in enumerate((gate_ref, up_ref)):
            out_refs[m][side] = ref[to // 2, :, :, at]


def place_kernel(own_ref, *refs):
    for m in range(4):
        refs[4][:, :, own_ref[0] ^ m] = refs[m][...]


def halves_kernel(f_ref, b_ref, f_out, b_out):
    f_out[...] = f_ref[...]
    b_out[...] = b_ref[...]


def block_of_rows(own_refs, partner_refs, j, m, x_lo, start, width):
    blk = partner_refs[0].shape[1]
    rows = own_refs[0].shape[0]
    if j < 2 and m < 2:
        return own_refs[m][:, pl.ds(pl.multiple_of((x_lo ^ j) * blk + start, 128), width)]
    column = pl.ds(pl.multiple_of(start, 128), width)
    if j < 2:
        return own_refs[2 * m - 2 + j][:, column]
    if j < 4:
        return partner_refs[m % 2 * 4 + j - 2][pl.ds(m // 2 * rows, rows), column]
    return partner_refs[m % 2 * 4 + 2 + m // 2][:, column]


def last_window(z, z_count, share, blk, window):
    row = (z + z_count // 2) % z_count * share
    return row, jnp.minimum(row // 128 * 128, blk - window)


def ring_row(i, z, z_count, share):
    origin = z - (i + 1) // 2 if i % 2 else z + i // 2
    return pl.ds(pl.multiple_of((origin + z_count) % z_count * share, 16), share)


def lay_kernel(place_ref, *refs, z_count, n_w):
    w_refs, own_refs, partner_refs = refs[:n_w], refs[n_w : n_w + 6], refs[n_w + 6 : n_w + 14]
    x_ref, windows, w_out = refs[n_w + 14 :]
    x_lo, z = place_ref[5], place_ref[6]
    share, width = w_refs[0].shape[2:]
    rows, (blk, window) = own_refs[0].shape[0], (x_ref.shape[2], windows.shape[2])
    _, start = last_window(z, z_count, share, blk, window)
    for j in range(5):
        for m in range(4):
            at = pl.ds(m * rows, rows)
            x_ref[j, at] = block_of_rows(own_refs, partner_refs, j, m, x_lo, 0, blk)
            windows[j, at] = block_of_rows(own_refs, partner_refs, j, m, x_lo, start, window)
        for i in range(z_count):
            at = ring_row(i, z, z_count, share)
            for side in range(2):
                piece = w_refs[i][side, place_ref[j]] if i < n_w else jnp.zeros((share, width), w_out.dtype)
                w_out[j, at, side * width : (side + 1) * width] = piece


def lay(place, weights, own_rows, partner_rows):
    rows, features = own_rows[0].shape
    blk = features // 2
    share, width = weights[0].shape[2:]
    window = min(2 * 128 * ((share + 127) // 128), blk)
    shapes = [(5, 4 * rows, blk), (5, 4 * rows, window), (5, blk, 2 * width)]
    return pl.pallas_call(
        functools.partial(lay_kernel, z_count=blk // share, n_w=len(weights)),
        out_shape=[jax.ShapeDtypeStruct(shape, jnp.bfloat16) for shape in shapes],
        in_specs=[SMEM] + [VMEM] * (len(weights) + 14),
        out_specs=[VMEM] * 3,
        compiler_params=pltpu.CompilerParams(vmem_limit_bytes=LAY_BYTES),
        cost_estimate=pl.CostEstimate(flops=2**20, bytes_accessed=2**20, transcendentals=0),
    )(place, *weights, *own_rows, *partner_rows)


def early_kernel(place_ref, gs_ref, us_ref, x_ref, w_ref, below_ref, above_ref, acc, x_mem, w_mem, x_sem, w_sem, *, z_count):
    z = place_ref[6]
    blk, both = w_mem.shape[1:]
    share, width = blk // z_count, both // 2
    copies = []
    for j in range(5):
        copies.append(pltpu.make_async_copy(w_ref.at[j], w_mem.at[j], w_sem.at[j]))
        copies.append(pltpu.make_async_copy(x_ref.at[j], x_mem.at[j], x_sem.at[j]))
    for copy in copies:
        copy.start()
    for j in range(5):
        slot = place_ref[j]
        copies[2 * j].wait()
        for i, ref in ((z_count - 3, below_ref), (z_count - 2, above_ref)):
            at = ring_row(i, z, z_count, share)
            for side in range(2):
                w_mem[j, at, side * width : (side + 1) * width] = ref[side, slot]
        copies[2 * j + 1].wait()
        term = jnp.dot(x_mem[j], w_mem[j], preferred_element_type=jnp.float32)
        g, u = term[:, :width] * gs_ref[slot], term[:, width:] * us_ref[slot]
        if j == 0:
            acc[:, :width] = g
            acc[:, width:] = u
        else:
            acc[:, :width] += g
            acc[:, width:] += u


def early(place, gs, us, x, weights, below, above):
    slots, rows, blk = x.shape
    share, width = below.shape[2:]
    return pl.pallas_call(
        functools.partial(early_kernel, z_count=blk // share),
        out_shape=jax.ShapeDtypeStruct((rows, 2 * width), jnp.float32),
        in_specs=[SMEM] * 3 + [ANY] * 2 + [VMEM] * 2,
        out_specs=VMEM,
        scratch_shapes=[
            pltpu.VMEM(x.shape, jnp.bfloat16),
            pltpu.VMEM(weights.shape, jnp.bfloat16),
            pltpu.SemaphoreType.DMA((slots,)),
            pltpu.SemaphoreType.DMA((slots,)),
        ],
        compiler_params=pltpu.CompilerParams(vmem_limit_bytes=VMEM_BYTES),
        cost_estimate=pl.CostEstimate(flops=2**20, bytes_accessed=2**20, transcendentals=0),
    )(place, gs, us, x, weights, below, above)


def late_kernel(place_ref, gs_ref, us_ref, g_ref, u_ref, acc_ref, window_ref, near_ref, far_ref, w_mem, acc, *, z_count):
    z = place_ref[6]
    share, width = g_ref.shape[2:]
    slots, rows, window = window_ref.shape
    rows //= 2
    row, start = last_window(z, z_count, share, z_count * share, window)
    at = pl.ds(pl.multiple_of(row - start, 16), share)
    w_mem[...] = jnp.zeros_like(w_mem)
    for j in range(slots):
        slot = place_ref[j]
        w_mem[j, at, :width] = g_ref[0, slot]
        w_mem[j, at, width:] = u_ref[0, slot]
        term = jnp.dot(window_ref[j], w_mem[j], preferred_element_type=jnp.float32)
        before = acc_ref if j == 0 else acc
        acc[:, :width] = before[:, :width] + term[:, :width] * gs_ref[slot]
        acc[:, width:] = before[:, width:] + term[:, width:] * us_ref[slot]
    g = acc[:, :width]
    out = (g / (1.0 + jnp.exp(-g)) * acc[:, width:]).astype(jnp.bfloat16)
    near_ref[...] = out[:rows]
    far_ref[...] = out[rows:]


def late(place, gs, us, weights, acc, windows, z_count, first):
    slots, rows, window = windows.shape
    rows //= 4
    share, width = weights[0].shape[2:]
    return pl.pallas_call(
        functools.partial(late_kernel, z_count=z_count),
        out_shape=[jax.ShapeDtypeStruct((rows, width), jnp.bfloat16)] * 2,
        grid=(1,),
        in_specs=[SMEM] * 3
        + [pl.BlockSpec((1, slots, share, width), lambda i: (0, 0, 0, 0))] * 2
        + [
            pl.BlockSpec((2 * rows, 2 * width), lambda i: (first, 0)),
            pl.BlockSpec((slots, 2 * rows, window), lambda i: (0, first, 0)),
        ],
        out_specs=[pl.BlockSpec((rows, width), lambda i: (0, 0))] * 2,
        scratch_shapes=[
            pltpu.VMEM((slots, window, 2 * width), jnp.bfloat16),
            pltpu.VMEM((2 * rows, 2 * width), jnp.float32),
        ],
        compiler_params=pltpu.CompilerParams(vmem_limit_bytes=VMEM_BYTES),
        cost_estimate=pl.CostEstimate(
            flops=2 * 2 * 2 * rows * slots * window * width, bytes_accessed=4 * 2**20, transcendentals=2 * rows * width
        ),
    )(place, gs, us, *weights, acc, windows)


def latent_kernel(own_ref, lin_ref, *refs):
    pieces, hidden_ref, part_ref, total = refs[:4], refs[4], refs[5], refs[6]
    step = pl.program_id(0)
    for m in range(4):

        @pl.when(step == m)
        def _(m=m):
            piece = pieces[m][...]
            hidden_ref[...] = piece
            term = jnp.dot(piece, lin_ref[...], preferred_element_type=jnp.float32)
            if m > 0:
                term += total[...]
            if m < 3:
                total[...] = term
            else:
                part_ref[...] = term.astype(jnp.bfloat16)


def per_device(tokens, gate_weight, up_weight, gate_scale, up_scale, partners, latent_in, latent_out):
    rows, features = tokens.shape
    blocks, slots, share, blk = gate_weight.shape
    feat_count = lax.axis_size("feat")
    half = blk // 2
    feat, tok = lax.axis_index("feat"), lax.axis_index("tok")
    member, z = tok % GROUP, tok // GROUP
    x_lo, core = member // 2, member % 2
    block_id = feat * blocks + x_lo

    wanted = lax.dynamic_index_in_dim(partners, block_id, 0, keepdims=False)
    labels = block_id ^ jnp.array([0, 1, 2, 4, 8], jnp.int32)
    order = jnp.sum(jnp.where(labels[:, None] == wanted[None, :], jnp.arange(5, dtype=jnp.int32)[None, :], 0), axis=1)
    here = jnp.concatenate([order, jnp.stack([x_lo, z]).astype(jnp.int32)])
    gs = lax.dynamic_index_in_dim(gate_scale, x_lo, 0, keepdims=False)
    us = lax.dynamic_index_in_dim(up_scale, x_lo, 0, keepdims=False)

    own = member[None].astype(jnp.int32)
    packed = pl.pallas_call(
        pack_kernel,
        out_shape=[jax.ShapeDtypeStruct((2, slots, share, half), jnp.bfloat16)] * 4,
        in_specs=[SMEM, VMEM, VMEM],
        out_specs=[VMEM] * 4,
        compiler_params=pltpu.CompilerParams(vmem_limit_bytes=LAY_BYTES),
    )(own, gate_weight, up_weight)

    def place(got):
        shape = got[0].shape
        out = pl.pallas_call(
            place_kernel,
            out_shape=jax.ShapeDtypeStruct(shape[:2] + (4,) + shape[2:], jnp.bfloat16),
            in_specs=[SMEM] + [VMEM] * 4,
            out_specs=VMEM,
            compiler_params=pltpu.CompilerParams(vmem_limit_bytes=LAY_BYTES),
        )(own, *got)
        return out.reshape(shape[:2] + (4 * shape[2],) + shape[3:])

    def block_of(value, which):
        return lax.dynamic_slice(value, (0, which * blk), (rows, blk))

    def step(forward, back):
        return shifted(forward, 1), shifted(back, -1)

    far = [swapped(packed[m], "tok", m) for m in (2, 3)]
    near = swapped(packed[1], "tok", 1)
    w0 = place([packed[0], near, *far])
    barrier = lax.optimization_barrier
    first, other = block_of(tokens, x_lo), block_of(tokens, 1 - x_lo)
    p0_y1, p0_y2 = swapped(first, "feat", 2), swapped(first, "feat", 4)
    w0, other, later = barrier((w0, other, tokens))
    w1 = step(w0, w0)
    s2_own = swapped(other, "tok", 2)
    first, s2_own, p0_y1, p0_y2 = barrier((first, s2_own, p0_y1, p0_y2))
    s2_other = swapped(first, "tok", 2)
    p2_y1 = swapped(s2_own, "feat", 2)
    w1, s2_own, s2_other, p0_y1, p0_y2, p2_y1, first, later = barrier(
        (w1, s2_own, s2_other, p0_y1, p0_y2, p2_y1, first, later)
    )
    w2 = step(*w1)
    p_x = swapped(jnp.concatenate([first, s2_own]), "feat", 1)
    p2_y2 = swapped(s2_own, "feat", 4)
    s1 = swapped(later, "tok", 1)
    s1, s2_other = barrier((s1, s2_other))
    s3_other = swapped(s2_other, "tok", 1)
    p_y1 = jnp.concatenate([p0_y1, p2_y1])
    w2, p_x, p2_y2, p0_y2, p_y1, s2_own, s1, s3_other = barrier((w2, p_x, p2_y2, p0_y2, p_y1, s2_own, s1, s3_other))
    w3 = step(*w2)
    q_x = swapped(p_x, "tok", 1)
    q_y1 = swapped(p_y1, "tok", 1)
    q_y1, p0_y2 = barrier((q_y1, p0_y2))
    q0_y2 = swapped(p0_y2, "tok", 1)
    q2_y2 = swapped(p2_y2, "tok", 1)
    q2_y2, s2_own = barrier((q2_y2, s2_own))
    s3_own = swapped(s2_own, "tok", 1)
    partner_rows = [p_x, p_y1, p0_y2, p2_y2, q_x, q_y1, q0_y2, q2_y2]
    own_rows = [later, s1, s2_own, s2_other, s3_own, s3_other]
    x, windows, w_laid = lay(here, (w0, *w1, *w2), own_rows, partner_rows)
    w3, x, windows, w_laid = barrier((w3, x, windows, w_laid))
    half_shape = (1,) + w3[0].shape[1:]
    cut = pl.pallas_call(
        halves_kernel,
        grid=(1,),
        out_shape=[jax.ShapeDtypeStruct(half_shape, jnp.bfloat16)] * 2,
        in_specs=[pl.BlockSpec(half_shape, lambda i: (0, 0, 0, 0)), pl.BlockSpec(half_shape, lambda i: (1, 0, 0, 0))],
        out_specs=[pl.BlockSpec(half_shape, lambda i: (0, 0, 0, 0))] * 2,
        compiler_params=pltpu.CompilerParams(vmem_limit_bytes=SMALL_BYTES),
    )(*w3)
    w4 = step(*cut)

    acc = early(here, gs, us, x, w_laid, *w3)
    z_count = lax.axis_size("tok") // GROUP
    made = late(here, gs, us, w4, acc, windows, z_count, 1)
    far_hidden = [swapped(v, "tok", mask) for v, mask in zip(made, (2, 3))]
    made = late(here, gs, us, w4, acc, windows, z_count, 0)
    hidden_pieces = [made[0], swapped(made[1], "tok", 1), *far_hidden]
    rank = latent_in.shape[1]
    hidden, part = pl.pallas_call(
        latent_kernel,
        out_shape=(
            jax.ShapeDtypeStruct((rows, features), jnp.bfloat16),
            jax.ShapeDtypeStruct((rows, rank), jnp.bfloat16),
        ),
        grid_spec=pltpu.PrefetchScalarGridSpec(
            num_scalar_prefetch=1,
            grid=(4,),
            in_specs=[pl.BlockSpec((half, rank), lambda m, own: (own[0] ^ m, 0))]
            + [pl.BlockSpec((rows, half), lambda m, own: (0, 0))] * 4,
            out_specs=[
                pl.BlockSpec((rows, half), lambda m, own: (0, own[0] ^ m)),
                pl.BlockSpec((rows, rank), lambda m, own: (0, 0)),
            ],
            scratch_shapes=[pltpu.VMEM((rows, rank), jnp.float32)],
        ),
        compiler_params=pltpu.CompilerParams(vmem_limit_bytes=VMEM_BYTES),
        cost_estimate=pl.CostEstimate(flops=2 * rows * features * rank, bytes_accessed=4 * 2**20, transcendentals=0),
    )(own, latent_in, *hidden_pieces)

    parts = part.reshape(feat_count, rows // feat_count, -1)
    terms = lax.all_to_all(parts, "feat", 0, 0)
    mine = jnp.sum(terms.astype(jnp.float32), axis=0).astype(jnp.bfloat16)
    latent = lax.all_to_all(jnp.broadcast_to(mine[None], parts.shape), "feat", 0, 0).reshape(rows, -1)
    rank_term = jnp.dot(latent, latent_out, preferred_element_type=jnp.float32).astype(jnp.bfloat16)
    return hidden, rank_term


def solution(mesh):
    placed = (
        P("tok", "feat"),
        P("feat", None, "tok", None),
        P("feat", None, "tok", None),
        P("feat", None),
        P("feat", None),
        P(),
        P("feat", None),
        P(None, "feat"),
    )
    return jax.shard_map(
        per_device,
        mesh=mesh,
        in_specs=placed,
        out_specs=(P("tok", "feat"), P("tok", "feat")),
        check_vma=False,
    )
```

```python
import functools
import jax
import jax.numpy as jnp
from jax import lax
from jax.experimental import pallas as pl
from jax.experimental.pallas import tpu as pltpu
from jax.sharding import PartitionSpec as P

GROUP = 4
ANY = pl.BlockSpec(memory_space=pl.ANY)
SMEM = pl.BlockSpec(memory_space=pltpu.SMEM)
VMEM = pl.BlockSpec(memory_space=pltpu.VMEM)
VMEM_BYTES = 44 * 2**20
LAY_BYTES = 60 * 2**20
SMALL_BYTES = 16 * 2**20


def swapped(value, axis, mask):
    return lax.ppermute(value, axis, [(i, i ^ mask) for i in range(lax.axis_size(axis))])


def shifted(value, step):
    count = lax.axis_size("tok")
    return lax.ppermute(value, "tok", [(i, (i + step * GROUP) % count) for i in range(count)])


def pack_kernel(own_ref, gate_ref, up_ref, *out_refs):
    half = gate_ref.shape[3] // 2
    for m in range(4):
        to = own_ref[0] ^ m
        at = pl.ds(pl.multiple_of(to % 2 * half, 128), half)
        for side, ref in enumerate((gate_ref, up_ref)):
            out_refs[m][side] = ref[to // 2, :, :, at]


def place_kernel(own_ref, *refs):
    for m in range(4):
        refs[4][:, :, own_ref[0] ^ m] = refs[m][...]


def halves_kernel(f_ref, b_ref, f_out, b_out):
    f_out[...] = f_ref[...]
    b_out[...] = b_ref[...]


def block_of_rows(own_refs, partner_refs, j, m, x_lo, start, width):
    blk = partner_refs[0].shape[1]
    rows = own_refs[0].shape[0]
    if j < 2 and m < 2:
        return own_refs[m][:, pl.ds(pl.multiple_of((x_lo ^ j) * blk + start, 128), width)]
    column = pl.ds(pl.multiple_of(start, 128), width)
    if j < 2:
        return own_refs[2 * m - 2 + j][:, column]
    if j < 4:
        return partner_refs[m % 2 * 4 + j - 2][pl.ds(m // 2 * rows, rows), column]
    return partner_refs[m % 2 * 4 + 2 + m // 2][:, column]


def last_window(z, z_count, share, blk, window):
    row = (z + z_count // 2) % z_count * share
    return row, jnp.minimum(row // 128 * 128, blk - window)


def ring_row(i, z, z_count, share):
    origin = z - (i + 1) // 2 if i % 2 else z + i // 2
    return pl.ds(pl.multiple_of((origin + z_count) % z_count * share, 16), share)


def lay_kernel(place_ref, *refs, z_count, n_w):
    w_refs, own_refs, partner_refs = refs[:n_w], refs[n_w : n_w + 6], refs[n_w + 6 : n_w + 14]
    x_ref, windows, w_out = refs[n_w + 14 :]
    x_lo, z = place_ref[5], place_ref[6]
    share, width = w_refs[0].shape[2:]
    rows, (blk, window) = own_refs[0].shape[0], (x_ref.shape[2], windows.shape[2])
    _, start = last_window(z, z_count, share, blk, window)
    for j in range(5):
        for m in range(4):
            at = pl.ds(m * rows, rows)
            x_ref[j, at] = block_of_rows(own_refs, partner_refs, j, m, x_lo, 0, blk)
            windows[j, at] = block_of_rows(own_refs, partner_refs, j, m, x_lo, start, window)
        for i in range(z_count):
            at = ring_row(i, z, z_count, share)
            for side in range(2):
                piece = w_refs[i][side, place_ref[j]] if i < n_w else jnp.zeros((share, width), w_out.dtype)
                w_out[j, at, side * width : (side + 1) * width] = piece


def lay(place, weights, own_rows, partner_rows):
    rows, features = own_rows[0].shape
    blk = features // 2
    share, width = weights[0].shape[2:]
    window = min(2 * 128 * ((share + 127) // 128), blk)
    shapes = [(5, 4 * rows, blk), (5, 4 * rows, window), (5, blk, 2 * width)]
    return pl.pallas_call(
        functools.partial(lay_kernel, z_count=blk // share, n_w=len(weights)),
        out_shape=[jax.ShapeDtypeStruct(shape, jnp.bfloat16) for shape in shapes],
        in_specs=[SMEM] + [VMEM] * (len(weights) + 14),
        out_specs=[VMEM] * 3,
        compiler_params=pltpu.CompilerParams(vmem_limit_bytes=LAY_BYTES),
        cost_estimate=pl.CostEstimate(flops=2**20, bytes_accessed=2**20, transcendentals=0),
    )(place, *weights, *own_rows, *partner_rows)


def early_kernel(place_ref, gs_ref, us_ref, x_ref, w_ref, below_ref, above_ref, acc, x_mem, w_mem, x_sem, w_sem, *, z_count):
    z = place_ref[6]
    blk, both = w_mem.shape[1:]
    share, width = blk // z_count, both // 2
    copies = []
    for j in range(5):
        copies.append(pltpu.make_async_copy(w_ref.at[j], w_mem.at[j], w_sem.at[j]))
        copies.append(pltpu.make_async_copy(x_ref.at[j], x_mem.at[j], x_sem.at[j]))
    for copy in copies:
        copy.start()
    for j in range(5):
        slot = place_ref[j]
        copies[2 * j].wait()
        for i, ref in ((z_count - 3, below_ref), (z_count - 2, above_ref)):
            at = ring_row(i, z, z_count, share)
            for side in range(2):
                w_mem[j, at, side * width : (side + 1) * width] = ref[side, slot]
        copies[2 * j + 1].wait()
        term = jnp.dot(x_mem[j], w_mem[j], preferred_element_type=jnp.float32)
        g, u = term[:, :width] * gs_ref[slot], term[:, width:] * us_ref[slot]
        if j == 0:
            acc[:, :width] = g
            acc[:, width:] = u
        else:
            acc[:, :width] += g
            acc[:, width:] += u


def early(place, gs, us, x, weights, below, above):
    slots, rows, blk = x.shape
    share, width = below.shape[2:]
    return pl.pallas_call(
        functools.partial(early_kernel, z_count=blk // share),
        out_shape=jax.ShapeDtypeStruct((rows, 2 * width), jnp.float32),
        in_specs=[SMEM] * 3 + [ANY] * 2 + [VMEM] * 2,
        out_specs=VMEM,
        scratch_shapes=[
            pltpu.VMEM(x.shape, jnp.bfloat16),
            pltpu.VMEM(weights.shape, jnp.bfloat16),
            pltpu.SemaphoreType.DMA((slots,)),
            pltpu.SemaphoreType.DMA((slots,)),
        ],
        compiler_params=pltpu.CompilerParams(vmem_limit_bytes=VMEM_BYTES),
        cost_estimate=pl.CostEstimate(flops=2**20, bytes_accessed=2**20, transcendentals=0),
    )(place, gs, us, x, weights, below, above)


def late_kernel(place_ref, gs_ref, us_ref, g_ref, u_ref, acc_ref, window_ref, near_ref, far_ref, w_mem, acc, *, z_count):
    z = place_ref[6]
    share, width = g_ref.shape[2:]
    slots, rows, window = window_ref.shape
    rows //= 2
    row, start = last_window(z, z_count, share, z_count * share, window)
    at = pl.ds(pl.multiple_of(row - start, 16), share)
    w_mem[...] = jnp.zeros_like(w_mem)
    for j in range(slots):
        slot = place_ref[j]
        w_mem[j, at, :width] = g_ref[0, slot]
        w_mem[j, at, width:] = u_ref[0, slot]
        term = jnp.dot(window_ref[j], w_mem[j], preferred_element_type=jnp.float32)
        before = acc_ref if j == 0 else acc
        acc[:, :width] = before[:, :width] + term[:, :width] * gs_ref[slot]
        acc[:, width:] = before[:, width:] + term[:, width:] * us_ref[slot]
    g = acc[:, :width]
    out = (g / (1.0 + jnp.exp(-g)) * acc[:, width:]).astype(jnp.bfloat16)
    near_ref[...] = out[:rows]
    far_ref[...] = out[rows:]


def late(place, gs, us, weights, acc, windows, z_count, first):
    slots, rows, window = windows.shape
    rows //= 4
    share, width = weights[0].shape[2:]
    return pl.pallas_call(
        functools.partial(late_kernel, z_count=z_count),
        out_shape=[jax.ShapeDtypeStruct((rows, width), jnp.bfloat16)] * 2,
        grid=(1,),
        in_specs=[SMEM] * 3
        + [pl.BlockSpec((1, slots, share, width), lambda i: (0, 0, 0, 0))] * 2
        + [
            pl.BlockSpec((2 * rows, 2 * width), lambda i: (first, 0)),
            pl.BlockSpec((slots, 2 * rows, window), lambda i: (0, first, 0)),
        ],
        out_specs=[pl.BlockSpec((rows, width), lambda i: (0, 0))] * 2,
        scratch_shapes=[
            pltpu.VMEM((slots, window, 2 * width), jnp.bfloat16),
            pltpu.VMEM((2 * rows, 2 * width), jnp.float32),
        ],
        compiler_params=pltpu.CompilerParams(vmem_limit_bytes=VMEM_BYTES),
        cost_estimate=pl.CostEstimate(
            flops=2 * 2 * 2 * rows * slots * window * width, bytes_accessed=4 * 2**20, transcendentals=2 * rows * width
        ),
    )(place, gs, us, *weights, acc, windows)


def latent_kernel(own_ref, lin_ref, *refs):
    pieces, hidden_ref, out_refs, part = refs[:4], refs[4], refs[5:-1], refs[-1]
    width = pieces[0].shape[1]
    total = None
    for m in range(4):
        at = pl.ds(pl.multiple_of((own_ref[0] ^ m) * width, width), width)
        piece = pieces[m][...]
        hidden_ref[:, at] = piece
        term = jnp.dot(piece, lin_ref[at], preferred_element_type=jnp.float32)
        total = term if total is None else total + term
    part[...] = total
    share = part.shape[0] // len(out_refs)
    for m, ref in enumerate(out_refs):
        ref[...] = part[pl.ds(pl.multiple_of((own_ref[1] ^ m) * share, share), share)].astype(ref.dtype)


def rank_kernel(own_ref, lout_ref, *refs):
    pieces, out_ref, latent = refs[:-2], refs[-2], refs[-1]
    share = pieces[0].shape[0]
    for m, ref in enumerate(pieces):
        latent[pl.ds(pl.multiple_of((own_ref[1] ^ m) * share, share), share)] = ref[...]
    out_ref[...] = jnp.dot(latent[...], lout_ref[...], preferred_element_type=jnp.float32).astype(out_ref.dtype)


def per_device(tokens, gate_weight, up_weight, gate_scale, up_scale, partners, latent_in, latent_out):
    rows, features = tokens.shape
    blocks, slots, share, blk = gate_weight.shape
    feat_count = lax.axis_size("feat")
    half = blk // 2
    feat, tok = lax.axis_index("feat"), lax.axis_index("tok")
    member, z = tok % GROUP, tok // GROUP
    x_lo, core = member // 2, member % 2
    block_id = feat * blocks + x_lo

    wanted = lax.dynamic_index_in_dim(partners, block_id, 0, keepdims=False)
    labels = block_id ^ jnp.array([0, 1, 2, 4, 8], jnp.int32)
    order = jnp.sum(jnp.where(labels[:, None] == wanted[None, :], jnp.arange(5, dtype=jnp.int32)[None, :], 0), axis=1)
    here = jnp.concatenate([order, jnp.stack([x_lo, z]).astype(jnp.int32)])
    gs = lax.dynamic_index_in_dim(gate_scale, x_lo, 0, keepdims=False)
    us = lax.dynamic_index_in_dim(up_scale, x_lo, 0, keepdims=False)

    own = member[None].astype(jnp.int32)
    packed = pl.pallas_call(
        pack_kernel,
        out_shape=[jax.ShapeDtypeStruct((2, slots, share, half), jnp.bfloat16)] * 4,
        in_specs=[SMEM, VMEM, VMEM],
        out_specs=[VMEM] * 4,
        compiler_params=pltpu.CompilerParams(vmem_limit_bytes=LAY_BYTES),
    )(own, gate_weight, up_weight)

    def place(got):
        shape = got[0].shape
        out = pl.pallas_call(
            place_kernel,
            out_shape=jax.ShapeDtypeStruct(shape[:2] + (4,) + shape[2:], jnp.bfloat16),
            in_specs=[SMEM] + [VMEM] * 4,
            out_specs=VMEM,
            compiler_params=pltpu.CompilerParams(vmem_limit_bytes=LAY_BYTES),
        )(own, *got)
        return out.reshape(shape[:2] + (4 * shape[2],) + shape[3:])

    def block_of(value, which):
        return lax.dynamic_slice(value, (0, which * blk), (rows, blk))

    def step(forward, back):
        return shifted(forward, 1), shifted(back, -1)

    far = [swapped(packed[m], "tok", m) for m in (2, 3)]
    near = swapped(packed[1], "tok", 1)
    w0 = place([packed[0], near, *far])
    barrier = lax.optimization_barrier
    first, other = block_of(tokens, x_lo), block_of(tokens, 1 - x_lo)
    p0_y1, p0_y2 = swapped(first, "feat", 2), swapped(first, "feat", 4)
    w0, other, later = barrier((w0, other, tokens))
    w1 = step(w0, w0)
    s2_own = swapped(other, "tok", 2)
    first, s2_own, p0_y1, p0_y2 = barrier((first, s2_own, p0_y1, p0_y2))
    s2_other = swapped(first, "tok", 2)
    p2_y1 = swapped(s2_own, "feat", 2)
    w1, s2_own, s2_other, p0_y1, p0_y2, p2_y1, first, later = barrier(
        (w1, s2_own, s2_other, p0_y1, p0_y2, p2_y1, first, later)
    )
    w2 = step(*w1)
    p_x = swapped(jnp.concatenate([first, s2_own]), "feat", 1)
    p2_y2 = swapped(s2_own, "feat", 4)
    s1 = swapped(later, "tok", 1)
    s1, s2_other = barrier((s1, s2_other))
    s3_other = swapped(s2_other, "tok", 1)
    p_y1 = jnp.concatenate([p0_y1, p2_y1])
    w2, p_x, p2_y2, p0_y2, p_y1, s2_own, s1, s3_other = barrier((w2, p_x, p2_y2, p0_y2, p_y1, s2_own, s1, s3_other))
    w3 = step(*w2)
    q_x = swapped(p_x, "tok", 1)
    q_y1 = swapped(p_y1, "tok", 1)
    q_y1, p0_y2 = barrier((q_y1, p0_y2))
    q0_y2 = swapped(p0_y2, "tok", 1)
    q2_y2 = swapped(p2_y2, "tok", 1)
    q2_y2, s2_own = barrier((q2_y2, s2_own))
    s3_own = swapped(s2_own, "tok", 1)
    partner_rows = [p_x, p_y1, p0_y2, p2_y2, q_x, q_y1, q0_y2, q2_y2]
    own_rows = [later, s1, s2_own, s2_other, s3_own, s3_other]
    x, windows, w_laid = lay(here, (w0, *w1, *w2), own_rows, partner_rows)
    w3, x, windows, w_laid = barrier((w3, x, windows, w_laid))
    half_shape = (1,) + w3[0].shape[1:]
    cut = pl.pallas_call(
        halves_kernel,
        grid=(1,),
        out_shape=[jax.ShapeDtypeStruct(half_shape, jnp.bfloat16)] * 2,
        in_specs=[pl.BlockSpec(half_shape, lambda i: (0, 0, 0, 0)), pl.BlockSpec(half_shape, lambda i: (1, 0, 0, 0))],
        out_specs=[pl.BlockSpec(half_shape, lambda i: (0, 0, 0, 0))] * 2,
        compiler_params=pltpu.CompilerParams(vmem_limit_bytes=SMALL_BYTES),
    )(*w3)
    w4 = step(*cut)

    acc = early(here, gs, us, x, w_laid, *w3)
    z_count = lax.axis_size("tok") // GROUP
    made = late(here, gs, us, w4, acc, windows, z_count, 1)
    far_hidden = [swapped(v, "tok", mask) for v, mask in zip(made, (2, 3))]
    made = late(here, gs, us, w4, acc, windows, z_count, 0)
    hidden_pieces = [made[0], swapped(made[1], "tok", 1), *far_hidden]
    rank = latent_in.shape[1]
    y_count = feat_count // 2
    own = jnp.stack([member, feat // 2]).astype(jnp.int32)
    hidden, *terms = pl.pallas_call(
        latent_kernel,
        out_shape=[jax.ShapeDtypeStruct((rows, features), jnp.bfloat16)]
        + [jax.ShapeDtypeStruct((rows // y_count, rank), jnp.bfloat16)] * y_count,
        in_specs=[SMEM] + [VMEM] * 5,
        out_specs=[VMEM] * (1 + y_count),
        scratch_shapes=[pltpu.VMEM((rows, rank), jnp.float32)],
        compiler_params=pltpu.CompilerParams(vmem_limit_bytes=SMALL_BYTES),
        cost_estimate=pl.CostEstimate(flops=2 * rows * features * rank, bytes_accessed=4 * 2**20, transcendentals=0),
    )(own, latent_in, *hidden_pieces)

    def summed(values):
        return sum(v.astype(jnp.float32) for v in values).astype(jnp.bfloat16)

    mine = summed([terms[0]] + [swapped(terms[m], "feat", 2 * m) for m in range(1, y_count)])
    mine = summed([mine, swapped(mine, "feat", 1)])
    latents = [mine] + [swapped(mine, "feat", 2 * m) for m in range(1, y_count)]
    rank_term = pl.pallas_call(
        rank_kernel,
        out_shape=jax.ShapeDtypeStruct((rows, features), jnp.bfloat16),
        in_specs=[SMEM] + [VMEM] * (1 + y_count),
        out_specs=VMEM,
        scratch_shapes=[pltpu.VMEM((rows, rank), jnp.bfloat16)],
        compiler_params=pltpu.CompilerParams(vmem_limit_bytes=SMALL_BYTES),
        cost_estimate=pl.CostEstimate(flops=2 * rows * features * rank, bytes_accessed=4 * 2**20, transcendentals=0),
    )(own, latent_out, *latents)
    return hidden, rank_term


def solution(mesh):
    placed = (
        P("tok", "feat"),
        P("feat", None, "tok", None),
        P("feat", None, "tok", None),
        P("feat", None),
        P("feat", None),
        P(),
        P("feat", None),
        P(None, "feat"),
    )
    return jax.shard_map(
        per_device,
        mesh=mesh,
        in_specs=placed,
        out_specs=(P("tok", "feat"), P("tok", "feat")),
        check_vma=False,
    )
```

```python
import functools
import jax
import jax.numpy as jnp
from jax import lax
from jax.experimental import pallas as pl
from jax.experimental.pallas import tpu as pltpu
from jax.sharding import PartitionSpec as P

GROUP = 4
ANY = pl.BlockSpec(memory_space=pl.ANY)
SMEM = pl.BlockSpec(memory_space=pltpu.SMEM)
VMEM = pl.BlockSpec(memory_space=pltpu.VMEM)
VMEM_BYTES = 44 * 2**20
LAY_BYTES = 60 * 2**20
SMALL_BYTES = 16 * 2**20


def swapped(value, axis, mask):
    return lax.ppermute(value, axis, [(i, i ^ mask) for i in range(lax.axis_size(axis))])


def shifted(value, step):
    count = lax.axis_size("tok")
    return lax.ppermute(value, "tok", [(i, (i + step * GROUP) % count) for i in range(count)])


def pack_kernel(own_ref, gate_ref, up_ref, *out_refs):
    half = gate_ref.shape[3] // 2
    for m in range(4):
        to = own_ref[0] ^ m
        at = pl.ds(pl.multiple_of(to % 2 * half, 128), half)
        for side, ref in enumerate((gate_ref, up_ref)):
            out_refs[m][side] = ref[to // 2, :, :, at]


def place_kernel(own_ref, *refs):
    for m in range(4):
        refs[4][:, :, own_ref[0] ^ m] = refs[m][...]


def halves_kernel(f_ref, b_ref, f_out, b_out):
    f_out[...] = f_ref[...]
    b_out[...] = b_ref[...]


def block_of_rows(own_refs, partner_refs, j, m, x_lo, start, width):
    blk = partner_refs[0].shape[1]
    rows = own_refs[0].shape[0]
    if j < 2 and m < 2:
        return own_refs[m][:, pl.ds(pl.multiple_of((x_lo ^ j) * blk + start, 128), width)]
    column = pl.ds(pl.multiple_of(start, 128), width)
    if j < 2:
        return own_refs[2 * m - 2 + j][:, column]
    if j < 4:
        return partner_refs[m % 2 * 4 + j - 2][pl.ds(m // 2 * rows, rows), column]
    return partner_refs[m % 2 * 4 + 2 + m // 2][:, column]


def last_window(z, z_count, share, blk, window):
    row = (z + z_count // 2) % z_count * share
    return row, jnp.minimum(row // 128 * 128, blk - window)


def ring_row(i, z, z_count, share):
    origin = z - (i + 1) // 2 if i % 2 else z + i // 2
    return pl.ds(pl.multiple_of((origin + z_count) % z_count * share, 16), share)


def lay_kernel(place_ref, *refs, z_count, n_w):
    w_refs, own_refs, partner_refs = refs[:n_w], refs[n_w : n_w + 6], refs[n_w + 6 : n_w + 14]
    x_ref, windows, w_out = refs[n_w + 14 :]
    x_lo, z = place_ref[5], place_ref[6]
    share, width = w_refs[0].shape[2:]
    rows, (blk, window) = own_refs[0].shape[0], (x_ref.shape[2], windows.shape[2])
    _, start = last_window(z, z_count, share, blk, window)
    for j in range(5):
        for m in range(4):
            at = pl.ds(m * rows, rows)
            x_ref[j, at] = block_of_rows(own_refs, partner_refs, j, m, x_lo, 0, blk)
            windows[j, at] = block_of_rows(own_refs, partner_refs, j, m, x_lo, start, window)
        for i in range(z_count):
            at = ring_row(i, z, z_count, share)
            for side in range(2):
                piece = w_refs[i][side, place_ref[j]] if i < n_w else jnp.zeros((share, width), w_out.dtype)
                w_out[j, at, side * width : (side + 1) * width] = piece


def lay(place, weights, own_rows, partner_rows):
    rows, features = own_rows[0].shape
    blk = features // 2
    share, width = weights[0].shape[2:]
    window = min(2 * 128 * ((share + 127) // 128), blk)
    shapes = [(5, 4 * rows, blk), (5, 4 * rows, window), (5, blk, 2 * width)]
    return pl.pallas_call(
        functools.partial(lay_kernel, z_count=blk // share, n_w=len(weights)),
        out_shape=[jax.ShapeDtypeStruct(shape, jnp.bfloat16) for shape in shapes],
        in_specs=[SMEM] + [VMEM] * (len(weights) + 14),
        out_specs=[VMEM] * 3,
        compiler_params=pltpu.CompilerParams(vmem_limit_bytes=LAY_BYTES),
        cost_estimate=pl.CostEstimate(flops=2**20, bytes_accessed=2**20, transcendentals=0),
    )(place, *weights, *own_rows, *partner_rows)


def early_kernel(place_ref, gs_ref, us_ref, x_ref, w_ref, below_ref, above_ref, acc, x_mem, w_mem, x_sem, w_sem, *, z_count):
    z = place_ref[6]
    blk, both = w_mem.shape[1:]
    share, width = blk // z_count, both // 2
    copies = []
    for j in range(5):
        copies.append(pltpu.make_async_copy(w_ref.at[j], w_mem.at[j], w_sem.at[j]))
        copies.append(pltpu.make_async_copy(x_ref.at[j], x_mem.at[j], x_sem.at[j]))
    for copy in copies:
        copy.start()
    for j in range(5):
        slot = place_ref[j]
        copies[2 * j].wait()
        for i, ref in ((z_count - 3, below_ref), (z_count - 2, above_ref)):
            at = ring_row(i, z, z_count, share)
            for side in range(2):
                w_mem[j, at, side * width : (side + 1) * width] = ref[side, slot]
        copies[2 * j + 1].wait()
        term = jnp.dot(x_mem[j], w_mem[j], preferred_element_type=jnp.float32)
        g, u = term[:, :width] * gs_ref[slot], term[:, width:] * us_ref[slot]
        if j == 0:
            acc[:, :width] = g
            acc[:, width:] = u
        else:
            acc[:, :width] += g
            acc[:, width:] += u


def early(place, gs, us, x, weights, below, above):
    slots, rows, blk = x.shape
    share, width = below.shape[2:]
    return pl.pallas_call(
        functools.partial(early_kernel, z_count=blk // share),
        out_shape=jax.ShapeDtypeStruct((rows, 2 * width), jnp.float32),
        in_specs=[SMEM] * 3 + [ANY] * 2 + [VMEM] * 2,
        out_specs=VMEM,
        scratch_shapes=[
            pltpu.VMEM(x.shape, jnp.bfloat16),
            pltpu.VMEM(weights.shape, jnp.bfloat16),
            pltpu.SemaphoreType.DMA((slots,)),
            pltpu.SemaphoreType.DMA((slots,)),
        ],
        compiler_params=pltpu.CompilerParams(vmem_limit_bytes=VMEM_BYTES),
        cost_estimate=pl.CostEstimate(flops=2**20, bytes_accessed=2**20, transcendentals=0),
    )(place, gs, us, x, weights, below, above)


def late_kernel(place_ref, gs_ref, us_ref, g_ref, u_ref, acc_ref, window_ref, near_ref, far_ref, w_mem, acc, *, z_count):
    z = place_ref[6]
    share, width = g_ref.shape[2:]
    slots, rows, window = window_ref.shape
    rows //= 2
    row, start = last_window(z, z_count, share, z_count * share, window)
    at = pl.ds(pl.multiple_of(row - start, 16), share)
    w_mem[...] = jnp.zeros_like(w_mem)
    for j in range(slots):
        slot = place_ref[j]
        w_mem[j, at, :width] = g_ref[0, slot]
        w_mem[j, at, width:] = u_ref[0, slot]
        term = jnp.dot(window_ref[j], w_mem[j], preferred_element_type=jnp.float32)
        before = acc_ref if j == 0 else acc
        acc[:, :width] = before[:, :width] + term[:, :width] * gs_ref[slot]
        acc[:, width:] = before[:, width:] + term[:, width:] * us_ref[slot]
    g = acc[:, :width]
    out = (g / (1.0 + jnp.exp(-g)) * acc[:, width:]).astype(jnp.bfloat16)
    near_ref[...] = out[:rows]
    far_ref[...] = out[rows:]


def late(place, gs, us, weights, acc, windows, z_count, first):
    slots, rows, window = windows.shape
    rows //= 4
    share, width = weights[0].shape[2:]
    return pl.pallas_call(
        functools.partial(late_kernel, z_count=z_count),
        out_shape=[jax.ShapeDtypeStruct((rows, width), jnp.bfloat16)] * 2,
        grid=(1,),
        in_specs=[SMEM] * 3
        + [pl.BlockSpec((1, slots, share, width), lambda i: (0, 0, 0, 0))] * 2
        + [
            pl.BlockSpec((2 * rows, 2 * width), lambda i: (first, 0)),
            pl.BlockSpec((slots, 2 * rows, window), lambda i: (0, first, 0)),
        ],
        out_specs=[pl.BlockSpec((rows, width), lambda i: (0, 0))] * 2,
        scratch_shapes=[
            pltpu.VMEM((slots, window, 2 * width), jnp.bfloat16),
            pltpu.VMEM((2 * rows, 2 * width), jnp.float32),
        ],
        compiler_params=pltpu.CompilerParams(vmem_limit_bytes=VMEM_BYTES),
        cost_estimate=pl.CostEstimate(
            flops=2 * 2 * 2 * rows * slots * window * width, bytes_accessed=4 * 2**20, transcendentals=2 * rows * width
        ),
    )(place, gs, us, *weights, acc, windows)


def latent_kernel(own_ref, lin_ref, *refs):
    pieces, hidden_ref, out_refs, part = refs[:4], refs[4], refs[5:-1], refs[-1]
    width = pieces[0].shape[1]
    total = None
    for m in range(4):
        at = pl.ds(pl.multiple_of((own_ref[0] ^ m) * width, width), width)
        piece = pieces[m][...]
        hidden_ref[:, at] = piece
        term = jnp.dot(piece, lin_ref[at], preferred_element_type=jnp.float32)
        total = term if total is None else total + term
    part[...] = total
    share = part.shape[0] // len(out_refs)
    for m, ref in enumerate(out_refs):
        ref[...] = part[pl.ds(pl.multiple_of((own_ref[1] ^ m) * share, share), share)].astype(ref.dtype)


def rank_kernel(own_ref, lout_ref, *refs):
    pieces, out_ref, latent = refs[:-2], refs[-2], refs[-1]
    share = pieces[0].shape[0]
    for m, ref in enumerate(pieces):
        latent[pl.ds(pl.multiple_of((own_ref[1] ^ m) * share, share), share)] = ref[...]
    out_ref[...] = jnp.dot(latent[...], lout_ref[...], preferred_element_type=jnp.float32).astype(out_ref.dtype)


def per_device(tokens, gate_weight, up_weight, gate_scale, up_scale, partners, latent_in, latent_out):
    rows, features = tokens.shape
    blocks, slots, share, blk = gate_weight.shape
    feat_count = lax.axis_size("feat")
    half = blk // 2
    feat, tok = lax.axis_index("feat"), lax.axis_index("tok")
    member, z = tok % GROUP, tok // GROUP
    x_lo, core = member // 2, member % 2
    block_id = feat * blocks + x_lo

    wanted = lax.dynamic_index_in_dim(partners, block_id, 0, keepdims=False)
    labels = block_id ^ jnp.array([0, 1, 2, 4, 8], jnp.int32)
    order = jnp.sum(jnp.where(labels[:, None] == wanted[None, :], jnp.arange(5, dtype=jnp.int32)[None, :], 0), axis=1)
    here = jnp.concatenate([order, jnp.stack([x_lo, z]).astype(jnp.int32)])
    gs = lax.dynamic_index_in_dim(gate_scale, x_lo, 0, keepdims=False)
    us = lax.dynamic_index_in_dim(up_scale, x_lo, 0, keepdims=False)

    own = member[None].astype(jnp.int32)
    packed = pl.pallas_call(
        pack_kernel,
        out_shape=[jax.ShapeDtypeStruct((2, slots, share, half), jnp.bfloat16)] * 4,
        in_specs=[SMEM, VMEM, VMEM],
        out_specs=[VMEM] * 4,
        compiler_params=pltpu.CompilerParams(vmem_limit_bytes=LAY_BYTES),
    )(own, gate_weight, up_weight)

    def place(got):
        shape = got[0].shape
        out = pl.pallas_call(
            place_kernel,
            out_shape=jax.ShapeDtypeStruct(shape[:2] + (4,) + shape[2:], jnp.bfloat16),
            in_specs=[SMEM] + [VMEM] * 4,
            out_specs=VMEM,
            compiler_params=pltpu.CompilerParams(vmem_limit_bytes=LAY_BYTES),
        )(own, *got)
        return out.reshape(shape[:2] + (4 * shape[2],) + shape[3:])

    def block_of(value, which):
        return lax.dynamic_slice(value, (0, which * blk), (rows, blk))

    def step(forward, back):
        return shifted(forward, 1), shifted(back, -1)

    far = [swapped(packed[m], "tok", m) for m in (2, 3)]
    near = swapped(packed[1], "tok", 1)
    w0 = place([packed[0], near, *far])
    barrier = lax.optimization_barrier
    first, other = block_of(tokens, x_lo), block_of(tokens, 1 - x_lo)
    p0_y1, p0_y2 = swapped(first, "feat", 2), swapped(first, "feat", 4)
    w0, other, later = barrier((w0, other, tokens))
    w1 = step(w0, w0)
    s2_own = swapped(other, "tok", 2)
    first, s2_own, p0_y1, p0_y2 = barrier((first, s2_own, p0_y1, p0_y2))
    s2_other = swapped(first, "tok", 2)
    p2_y1 = swapped(s2_own, "feat", 2)
    w1, s2_own, s2_other, p0_y1, p0_y2, p2_y1, first, later = barrier(
        (w1, s2_own, s2_other, p0_y1, p0_y2, p2_y1, first, later)
    )
    w2 = step(*w1)
    p_x = swapped(jnp.concatenate([first, s2_own]), "feat", 1)
    p2_y2 = swapped(s2_own, "feat", 4)
    s3_other = swapped(s2_other, "tok", 1)
    s3_other, later = barrier((s3_other, later))
    s1 = swapped(later, "tok", 1)
    p_y1 = jnp.concatenate([p0_y1, p2_y1])
    w2, p_x, p2_y2, p0_y2, p_y1, s2_own, s1, s3_other = barrier((w2, p_x, p2_y2, p0_y2, p_y1, s2_own, s1, s3_other))
    w3 = step(*w2)
    q_x = swapped(p_x, "tok", 1)
    q_y1 = swapped(p_y1, "tok", 1)
    q_y1, p0_y2 = barrier((q_y1, p0_y2))
    q0_y2 = swapped(p0_y2, "tok", 1)
    q2_y2 = swapped(p2_y2, "tok", 1)
    q2_y2, s2_own = barrier((q2_y2, s2_own))
    s3_own = swapped(s2_own, "tok", 1)
    partner_rows = [p_x, p_y1, p0_y2, p2_y2, q_x, q_y1, q0_y2, q2_y2]
    own_rows = [later, s1, s2_own, s2_other, s3_own, s3_other]
    x, windows, w_laid = lay(here, (w0, *w1, *w2), own_rows, partner_rows)
    w3, x, windows, w_laid = barrier((w3, x, windows, w_laid))
    half_shape = (1,) + w3[0].shape[1:]
    cut = pl.pallas_call(
        halves_kernel,
        grid=(1,),
        out_shape=[jax.ShapeDtypeStruct(half_shape, jnp.bfloat16)] * 2,
        in_specs=[pl.BlockSpec(half_shape, lambda i: (0, 0, 0, 0)), pl.BlockSpec(half_shape, lambda i: (1, 0, 0, 0))],
        out_specs=[pl.BlockSpec(half_shape, lambda i: (0, 0, 0, 0))] * 2,
        compiler_params=pltpu.CompilerParams(vmem_limit_bytes=SMALL_BYTES),
    )(*w3)
    w4 = step(*cut)

    acc = early(here, gs, us, x, w_laid, *w3)
    z_count = lax.axis_size("tok") // GROUP
    made = late(here, gs, us, w4, acc, windows, z_count, 1)
    far_hidden = [swapped(v, "tok", mask) for v, mask in zip(made, (2, 3))]
    made = late(here, gs, us, w4, acc, windows, z_count, 0)
    hidden_pieces = [made[0], swapped(made[1], "tok", 1), *far_hidden]
    rank = latent_in.shape[1]
    y_count = feat_count // 2
    own = jnp.stack([member, feat // 2]).astype(jnp.int32)
    hidden, *terms = pl.pallas_call(
        latent_kernel,
        out_shape=[jax.ShapeDtypeStruct((rows, features), jnp.bfloat16)]
        + [jax.ShapeDtypeStruct((rows // y_count, rank), jnp.bfloat16)] * y_count,
        in_specs=[SMEM] + [VMEM] * 5,
        out_specs=[VMEM] * (1 + y_count),
        scratch_shapes=[pltpu.VMEM((rows, rank), jnp.float32)],
        compiler_params=pltpu.CompilerParams(vmem_limit_bytes=SMALL_BYTES),
        cost_estimate=pl.CostEstimate(flops=2 * rows * features * rank, bytes_accessed=4 * 2**20, transcendentals=0),
    )(own, latent_in, *hidden_pieces)

    def summed(values):
        return sum(v.astype(jnp.float32) for v in values).astype(jnp.bfloat16)

    mine = summed([terms[0]] + [swapped(terms[m], "feat", 2 * m) for m in range(1, y_count)])
    mine = summed([mine, swapped(mine, "feat", 1)])
    latents = [mine] + [swapped(mine, "feat", 2 * m) for m in range(1, y_count)]
    rank_term = pl.pallas_call(
        rank_kernel,
        out_shape=jax.ShapeDtypeStruct((rows, features), jnp.bfloat16),
        in_specs=[SMEM] + [VMEM] * (1 + y_count),
        out_specs=VMEM,
        scratch_shapes=[pltpu.VMEM((rows, rank), jnp.bfloat16)],
        compiler_params=pltpu.CompilerParams(vmem_limit_bytes=SMALL_BYTES),
        cost_estimate=pl.CostEstimate(flops=2 * rows * features * rank, bytes_accessed=4 * 2**20, transcendentals=0),
    )(own, latent_out, *latents)
    return hidden, rank_term


def solution(mesh):
    placed = (
        P("tok", "feat"),
        P("feat", None, "tok", None),
        P("feat", None, "tok", None),
        P("feat", None),
        P("feat", None),
        P(),
        P("feat", None),
        P(None, "feat"),
    )
    return jax.shard_map(
        per_device,
        mesh=mesh,
        in_specs=placed,
        out_specs=(P("tok", "feat"), P("tok", "feat")),
        check_vma=False,
    )
```
